768 devices in a mesh: lon: 24 (over z_lo, x, core), lat: 32 (over z_hi, y).
Axes of the slice: x: 4, y: 8, z: 12 (z_hi: 4, z_lo: 3; z = z_hi * 3 + z_lo), core: 2. Of those that a mesh axis runs over, the one named last changes fastest.
Arguments:
- innovation: bfloat16 [64, 1179648], P(None, ('lon', 'lat')), may hold values from -6 to 6
- owner_tile: int32 [1179648, 1], P(('lon', 'lat')), may hold values from 0 to 23; in each aligned block of 1536 rows (0 to 1535, 1536 to 3071, ...) at most 128 rows name the same one
- cell_index: int32 [1179648], P(('lon', 'lat')), may hold values from 0 to 8191
- length_scale: float32 [64], replicated, may hold values from 1.5 to 8
- eof_basis: bfloat16 [137, 64], replicated, may hold values from -0.75 to 0.75
Outputs:
- increment: bfloat16 [137, 2048, 3072], P(None, 'lat', 'lon')
The draws below stay inside these ranges and needn't reach their ends.
Inputs may be any that keep to these rules, and one draw needn't show every extreme that they name: `owner_tile`: within the rows of one device (1536 rows, aligned blocks), no tile index appears more than 128 times, and some index appears exactly 128 times.
All inputs are finite; a program needn't handle non-finite values.
Results may differ from the reference program's by a relative error of at most 0.0076.
Values may be sent and summed in bfloat16 or wider, within the bound.
No kernel may reach another device: no remote copies, remote signals or barrier semaphores. Data moves between devices by JAX's collectives and lax.ppermute only.
A program may use at most 64 MiB of HBM per device.

```python
import math
import jax
import jax.numpy as jnp
import numpy as np
from jax import lax

LEV = 64
LEVELS = 137
TX = 128
TY = 64
REC = 1536
CAP = 128
NX = 3072
NY = 2048
OBS = 1179648
N_LON = 24
N_LAT = 32


def set_ends(result, key, low, top_value):
    longest = result.shape.index(max(result.shape))
    spots = []
    for shift in (0, 1):
        where = [jax.random.randint(jax.random.fold_in(key, axis), (), 0, length) for axis, length in enumerate(result.shape)]
        where[longest] = (where[longest] + shift) % result.shape[longest]
        spots.append(tuple(where))
    return result.at[spots[0]].set(low).at[spots[1]].set(top_value)


def level_of(stream_key, shape, shards, low, high):
    def one(axis_at, parts):
        heights = jax.random.uniform(jax.random.fold_in(jax.random.fold_in(stream_key, 6), axis_at), (parts,), jnp.float32, low / len(shards), high / len(shards))
        return jnp.repeat(jnp.exp(heights), shape[axis_at] // parts).reshape((-1,) + (1,) * (len(shape) - axis_at - 1))

    loudness = one(*shards[0])
    for cut in shards[1:]:
        loudness = loudness * one(*cut)
    return loudness


def assign_block(own_key, own, number, rows, number_of, top, most, lean):
    order = jax.random.permutation(own_key, number_of)
    crowded, ordinary = portions_of(number_of, rows * top, most, lean, True), portions_of(number_of, rows * top, most, lean, False)
    places = jnp.arange(number_of)

    def named(lengths, turn):
        used = int((lengths > 0).sum())
        fixed = max(1, used // 4)
        moved = fixed + (places - fixed + turn * (used - fixed)) % max(1, number_of - fixed)
        return jnp.zeros((number_of,), jnp.int32).at[order[jnp.where(places < fixed, places, moved)]].set(jnp.asarray(lengths, jnp.int32))

    lengths = jnp.where(number % 4 == 0, named(crowded, number // 4), named(ordinary, number - number // 4 - 1))
    mixed = jax.random.permutation(jax.random.fold_in(own, 3), number_of)
    donor, receiver = mixed[0:number_of // 2 * 2:2], mixed[1:number_of // 2 * 2:2]
    margin = jnp.minimum(lengths[donor] - 1, most - lengths[receiver]) // 2
    margin = jnp.where((donor == order[0]) | (receiver == order[0]) | (lengths[receiver] == 0), 0, jnp.maximum(margin, 0))
    moved = jax.random.randint(jax.random.fold_in(own, 4), (number_of // 2,), 0, 1 << 20) % (margin + 1)
    lengths = lengths.at[donor].add(-moved).at[receiver].add(moved)
    labels = jnp.searchsorted(jnp.cumsum(lengths), jnp.arange(rows * top), side="right").astype(jnp.int32)
    table = labels.reshape(top, rows).T
    table = table[jax.random.permutation(jax.random.fold_in(own, 1), rows)]
    turn = jax.random.randint(jax.random.fold_in(own, 2), (rows, 1), 0, top)
    return jnp.take_along_axis(table, (jnp.arange(top)[None, :] + turn) % top, axis=1)


def portions_of(number_of, total, most, slope, full):
    loads = [(1 << 20) // math.isqrt(grade ** slope) + 1 for grade in range(1, number_of + 1)]
    largest = most if full else min(most, max(-(-total // number_of), total * loads[0] // sum(loads)))
    least = 1 if total - largest >= number_of - 1 else 0
    counts, surplus = [largest] + [least] * (number_of - 1), total - largest - least * (number_of - 1)
    while surplus > 0:
        free = [i for i in range(1, number_of) if counts[i] < largest] or [i for i in range(1, number_of) if counts[i] < most]
        whole, budget = sum([loads[i] for i in free]), surplus
        for i in free:
            addition = min(most - counts[i], max(1, budget * loads[i] // whole), surplus)
            counts[i] = counts[i] + addition
            surplus = surplus - addition
    return np.array(counts)


def bell_draw(own_key, shape, scale, bound, cuts=(), kind=jnp.bfloat16):
    entries = jax.random.normal(own_key, shape, jnp.float32) * scale
    if len(cuts) > 0:
        entries = level_of(own_key, shape, cuts, -0.22, 0.18) * entries
    return jnp.clip(entries, min=-bound, max=bound).astype(kind)


def setup_inputs(seed: int = 0) -> dict:
    arg_keys = jax.random.split(jax.random.key(seed), 6)
    innovation = bell_draw(arg_keys[0], (LEV, OBS), 1.0, 6.0, ((1, 768),))
    owner_tile_keys = jax.random.split(jax.random.fold_in(arg_keys[1], 1), OBS // REC)
    owner_tile_turns = jax.random.permutation(jax.random.fold_in(arg_keys[1], 3), OBS // REC)
    owner_tile = jax.vmap(lambda own, number: assign_block(jax.random.fold_in(arg_keys[1], 2), own, number, REC, N_LON, 1, CAP, 2))(owner_tile_keys, owner_tile_turns).reshape((OBS, 1))
    cell_index = set_ends(jax.random.randint(arg_keys[2], (OBS,), 0, TX * TY), jax.random.fold_in(arg_keys[2], 1), 0, (TX * TY) - 1).astype(jnp.int32)
    length_scale = jnp.clip(jnp.exp(jax.random.uniform(arg_keys[3], (LEV,), jnp.float32, math.log(1.5), math.log(8.0))), 1.5, 8.0)
    eof_basis = bell_draw(arg_keys[4], (LEVELS, LEV), LEV ** -0.5, 0.75)
    return {"innovation": innovation, "owner_tile": owner_tile, "cell_index": cell_index, "length_scale": length_scale, "eof_basis": eof_basis}


def tap_norm(scale):
    dist = jnp.arange(-15, 16).astype(jnp.float32)
    gauss = jnp.exp(-(dist[None, :] * dist[None, :]) / (2.0 * scale[:, None] * scale[:, None]))
    return jnp.sqrt(lax.optimization_barrier(jnp.sum(gauss * gauss, axis=1)))

def tap_weight(dist, scale, norm):
    value = jnp.exp(-(dist * dist) / (2.0 * scale * scale)) / norm
    return jnp.where(jnp.abs(dist) <= 15.0, value, 0.0)

def lon_pass(plane, wts):
    total = jnp.zeros(plane.shape, jnp.float32)
    for index in range(31):
        shift = index - 15
        total = total + wts[index].astype(jnp.float32) * jnp.roll(plane, -shift, axis=1).astype(jnp.float32)
    return total.astype(jnp.bfloat16)

def lat_pass(plane, wts):
    padded = jnp.pad(plane, ((15, 15), (0, 0)))
    total = jnp.zeros(plane.shape, jnp.float32)
    for index in range(31):
        total = total + wts[index].astype(jnp.float32) * padded[index:index + NY].astype(jnp.float32)
    return total.astype(jnp.bfloat16)

def reference(innovation, owner_tile, cell_index, length_scale, eof_basis):
    holder = jnp.arange(OBS, dtype=jnp.int32) // REC
    band = holder % N_LAT
    row_at = band * TY + cell_index // TX
    col_at = owner_tile[:, 0] * TX + cell_index % TX
    flat = (row_at * NX + col_at).astype(jnp.int32)
    sums = jax.ops.segment_sum(innovation.T.astype(jnp.float32), flat, num_segments=NY * NX)
    spread = sums.T.reshape(LEV, NY, NX).astype(jnp.bfloat16)
    norm = tap_norm(length_scale)
    dist = jnp.arange(-15, 16).astype(jnp.float32)
    table = tap_weight(dist[None, :], length_scale[:, None], norm[:, None]).astype(jnp.bfloat16)
    lon_smooth = lax.map(lambda pair: lon_pass(pair[0], pair[1]), (spread, table))
    lat_smooth = lax.map(lambda pair: lat_pass(pair[0], pair[1]), (lon_smooth, table))
    mixed = jnp.dot(eof_basis, lat_smooth.reshape(LEV, NY * NX), preferred_element_type=jnp.float32)
    return mixed.astype(jnp.bfloat16).reshape(LEVELS, NY, NX)
```

```python
import jax
import jax.numpy as jnp
from jax import lax
from jax.experimental import pallas as pl
from jax.experimental.pallas import tpu as pltpu
from jax.sharding import PartitionSpec as P

TX = 128
TY = 64
CAP = 128
HALO = 16
SLABS = 8
BF = jnp.bfloat16
F32 = jnp.float32
VMEM = pl.BlockSpec(memory_space=pltpu.VMEM)


def tap_table(scale):
    taps = jnp.arange(-15, 16).astype(F32)
    gauss = jnp.exp(-(taps[None, :] * taps[None, :]) / (2.0 * scale[:, None] * scale[:, None]))
    norm = jnp.sqrt(jnp.sum(gauss * gauss, axis=1))
    lane = jnp.arange(TX)
    dist = jnp.minimum(lane, TX - lane).astype(F32)[None, :]
    value = jnp.exp(-(dist * dist) / (2.0 * scale[:, None] * scale[:, None])) / norm[:, None]
    return jnp.where(dist <= 15.0, value, 0.0).astype(BF).astype(F32)


def iota(shape, dim):
    return lax.broadcasted_iota(jnp.int32, shape, dim)


def dot_nt(left, right):
    return lax.dot_general(left, right, (((1,), (1,)), ((), ())), preferred_element_type=F32)


def bucket_kernel(innov_ref, owner_ref, cell_ref, out_ref):
    lev, rec = innov_ref.shape
    n_dest = out_ref.shape[0]
    owner = owner_ref[...]
    cell = cell_ref[...]
    padded = (n_dest + 7) // 8 * 8
    hits = jnp.where(iota((padded, rec), 0) == owner, 1.0, 0.0).astype(F32)
    earlier = jnp.where(iota((CAP, CAP), 0) < iota((CAP, CAP), 1), 1.0, 0.0).astype(BF)
    carry = jnp.zeros((padded, 1), F32)
    ranks = []
    for block in range(rec // CAP):
        here = hits[:, block * CAP : (block + 1) * CAP]
        before = jnp.dot(here.astype(BF), earlier, preferred_element_type=F32) + carry
        ranks.append(jnp.sum(here * before, axis=0, keepdims=True))
        carry = carry + jnp.sum(here, axis=1, keepdims=True)
    rank = jnp.concatenate(ranks, axis=1)
    line = iota((16, rec), 0)
    coords = jnp.where(line == 0, cell >> 7, jnp.where(line == 1, cell & 127, 0))
    source = jnp.concatenate([innov_ref[...], coords.astype(F32).astype(BF)], axis=0)
    slot = iota((2 * CAP, rec), 0).astype(F32).astype(BF)

    @pl.loop(0, n_dest // 2)
    def _(pair):
        code = jnp.where(
            owner == 2 * pair, rank, jnp.where(owner == 2 * pair + 1, rank + float(CAP), -1.0)
        )
        onehot = jnp.where(slot == code.astype(BF), 1.0, 0.0).astype(BF)
        moved = dot_nt(source, onehot).astype(BF)
        out_ref[2 * pair] = moved[: lev + 2, :CAP]
        out_ref[2 * pair + 1] = moved[: lev + 2, CAP:]


def gather_records(got_ref, vals_ref):
    n_src, lines, cap = got_ref.shape
    lev = lines - 2
    rows, cols = [], []
    for src in range(n_src):
        vals_ref[:, src * cap : (src + 1) * cap] = got_ref[src, :lev, :]
        rows.append(got_ref[src, lev : lev + 1, :].astype(F32))
        cols.append(got_ref[src, lev + 1 : lev + 2, :].astype(F32))
    row = jnp.concatenate(rows, axis=1).astype(jnp.int32)
    col = jnp.concatenate(cols, axis=1).astype(jnp.int32)
    return row, col


def onehot_rows(code, ref):
    spot = iota(ref.shape, 0).astype(F32).astype(BF)
    ref[...] = jnp.where(spot == code.astype(F32).astype(BF), 1.0, 0.0).astype(BF)


def edge_kernel(got_ref, first_ref, last_ref, vals_ref, right_ref, left_ref, wide_ref):
    lev = vals_ref.shape[0]
    row, col = gather_records(got_ref, vals_ref)
    slab = row >> 3
    code = jnp.where(
        col < HALO,
        slab * HALO + col,
        jnp.where(col >= TX - HALO, TX + slab * HALO + col - (TX - HALO), -1),
    )
    onehot_rows(code, right_ref)
    vals = vals_ref[...]
    low = (row & 7).astype(F32).astype(BF)
    for part in range(SLABS):
        left_ref[part * lev : (part + 1) * lev, :] = vals * jnp.where(
            low == float(part), 1.0, 0.0
        ).astype(BF)
    total = dot_nt(left_ref[...], right_ref[...])
    for half, out_ref in enumerate((first_ref, last_ref)):
        for part in range(SLABS):
            wide_ref[pl.ds(part, lev, stride=SLABS), :] = total[
                part * lev : (part + 1) * lev, half * TX : (half + 1) * TX
            ]
        out_ref[...] = wide_ref[...].astype(BF)


def spread_kernel(got_ref, out_ref, vals_ref, right_ref, left_ref, low_ref, wide_ref):
    lev = vals_ref.shape[0]
    row, col = gather_records(got_ref, vals_ref)
    half_rows = TY // 2
    onehot_rows((row >> 5) * TX + col, right_ref)
    low_ref[...] = (row & (half_rows - 1)).astype(F32)

    @pl.loop(0, half_rows // SLABS)
    def _(block):
        vals = vals_ref[...]
        low = low_ref[...] - (block * SLABS).astype(F32)
        low = low.astype(BF)
        for part in range(SLABS):
            left_ref[part * lev : (part + 1) * lev, :] = vals * jnp.where(
                low == float(part), 1.0, 0.0
            ).astype(BF)
        total = dot_nt(left_ref[...], right_ref[...])
        for part in range(SLABS):
            piece = total[part * lev : (part + 1) * lev]
            at = block * SLABS + part
            wide_ref[pl.ds(at, lev, stride=TY), :] = piece[:, :TX]
            wide_ref[pl.ds(at + half_rows, lev, stride=TY), :] = piece[:, TX:]

    out_ref[...] = wide_ref[...].astype(BF)


def band_kernel(table_ref, lon_ref, lat_ref):
    near = jnp.abs(iota((TX, TX), 0) - iota((TX, TX), 1)) < TX // 2

    @pl.loop(0, table_ref.shape[0], unroll=4)
    def _(c):
        base = jnp.broadcast_to(table_ref[pl.ds(c, 1), :], (TX, TX))
        ring = pltpu.roll(base, 0, 1, stride=1, stride_axis=0)
        lon_ref[c, :TX, :] = jnp.where(near, ring, 0.0).astype(BF)
        lon_ref[c, TX:, :] = jnp.where(near, 0.0, ring).astype(BF)
        lat_ref[c] = ring[:TY].astype(BF)


def lon_smooth_one(c, slabs, own_ref, east_ref, west_ref, band_ref):
    east = east_ref[pl.ds(pl.multiple_of(c * SLABS, SLABS), SLABS), :].astype(F32)
    west = west_ref[pl.ds(pl.multiple_of(c * SLABS, SLABS), SLABS), :].astype(F32)
    lane = iota((SLABS, TX), 1)
    sides = []
    for slab in slabs:
        right = pltpu.roll(east, (TX - slab * HALO) % TX, 1)
        left = pltpu.roll(west, (TX - HALO - slab * HALO) % TX, 1)
        sides.append(jnp.where(lane < TX // 2, right, left))
    side = jnp.concatenate(sides, axis=0).astype(BF)
    own = jnp.concatenate(
        [
            own_ref[pl.ds(pl.multiple_of(c * TY + slab * 8, 16), 16), :]
            for slab in slabs
            if slab % 2 == 0
        ],
        axis=0,
    )
    both = jnp.concatenate([own, side], axis=1)
    return jnp.dot(both, band_ref[c], preferred_element_type=F32)


def lon_edge_kernel(own_ref, east_ref, west_ref, band_ref, top_ref, bottom_ref):
    @pl.loop(0, band_ref.shape[0], unroll=4)
    def _(c):
        out = lon_smooth_one(c, (0, 1, 6, 7), own_ref, east_ref, west_ref, band_ref).astype(BF)
        here = pl.ds(pl.multiple_of(c * HALO, HALO), HALO)
        top_ref[here, :] = out[:HALO]
        bottom_ref[here, :] = out[HALO:]


def lon_middle_kernel(own_ref, east_ref, west_ref, band_ref, middle_ref):
    @pl.loop(0, band_ref.shape[0], unroll=4)
    def _(c):
        out = lon_smooth_one(c, (2, 3, 4, 5), own_ref, east_ref, west_ref, band_ref).astype(BF)
        middle_ref[pl.ds(pl.multiple_of(c * 32, 32), 32), :] = out


def final_kernel(
    above_ref, top_ref, middle_ref, bottom_ref, below_ref, band_ref, eof_ref, out_ref, lat_ref, mix_ref
):
    lev = band_ref.shape[0]
    levels = eof_ref.shape[0]
    blank = jnp.zeros((TX - TY - 2 * HALO, TX), BF)

    @pl.loop(0, lev, unroll=4)
    def _(c):
        edge = pl.ds(pl.multiple_of(c * HALO, HALO), HALO)
        middle = pl.ds(pl.multiple_of(c * 32, 32), 32)
        field = jnp.concatenate(
            [
                top_ref[edge, :],
                middle_ref[middle, :],
                bottom_ref[edge, :],
                below_ref[edge, :],
                blank,
                above_ref[edge, :],
            ],
            axis=0,
        )
        lat_ref[pl.ds(c, TY, stride=lev), :] = jnp.dot(
            band_ref[c], field, preferred_element_type=F32
        )

    eof = eof_ref[...]

    @pl.loop(0, TY // 2, unroll=2)
    def _(pair):
        at = pl.multiple_of(pair * 2 * lev, 2 * lev)
        fields = jnp.concatenate(
            [lat_ref[pl.ds(at, lev), :], lat_ref[pl.ds(at + lev, lev), :]], axis=1
        )
        mixed = jnp.dot(eof, fields.astype(BF), preferred_element_type=F32)
        mix_ref[pl.ds(2 * pair, levels, stride=TY), :] = mixed[:, :TX]
        mix_ref[pl.ds(2 * pair + 1, levels, stride=TY), :] = mixed[:, TX:]

    @pl.loop(0, levels)
    def _(level):
        at = pl.multiple_of(level * TY, TY)
        out_ref[level] = mix_ref[pl.ds(at, TY), :].astype(BF)


def call(kernel, outs, scratch, flops, moved, *args):
    return pl.pallas_call(
        kernel,
        out_shape=outs,
        in_specs=[VMEM] * len(args),
        out_specs=jax.tree.map(lambda _: VMEM, outs),
        scratch_shapes=scratch,
        compiler_params=pltpu.CompilerParams(vmem_limit_bytes=48 * 2**20),
        cost_estimate=pl.CostEstimate(flops=flops, bytes_accessed=moved, transcendentals=0),
    )(*args)


def local(innovation, owner_tile, cell_index, length_scale, eof_basis):
    n_lon = lax.axis_size("lon")
    n_lat = lax.axis_size("lat")
    lev, rec = innovation.shape
    levels = eof_basis.shape[0]
    slots = n_lon * CAP
    shape = jax.ShapeDtypeStruct
    sent = call(
        bucket_kernel,
        shape((n_lon, lev + 2, CAP), BF),
        [],
        2 * 80 * rec * slots,
        1 << 20,
        innovation,
        owner_tile.reshape(1, rec),
        cell_index.reshape(1, rec),
    )
    got = lax.all_to_all(sent, "lon", split_axis=0, concat_axis=0, tiled=True)
    table = tap_table(length_scale)
    band_lon, band_lat = call(
        band_kernel,
        (shape((lev, 2 * TX, TX), BF), shape((lev, TY, TX), BF)),
        [],
        1 << 20,
        6 << 20,
        table,
    )
    scratch = [
        pltpu.VMEM((lev, slots), BF),
        pltpu.VMEM((2 * TX, slots), BF),
        pltpu.VMEM((SLABS * lev, slots), BF),
    ]
    first, last = call(
        edge_kernel,
        (shape((lev * SLABS, TX), BF),) * 2,
        scratch + [pltpu.VMEM((lev * SLABS, TX), F32)],
        2 * SLABS * lev * slots * 2 * TX,
        1 << 20,
        got,
    )
    up = [(i, (i + 1) % n_lon) for i in range(n_lon)]
    down = [(j, i) for i, j in up]
    west = lax.ppermute(last, "lon", up)
    east = lax.ppermute(first, "lon", down)
    own = call(
        spread_kernel,
        shape((lev * TY, TX), BF),
        scratch + [pltpu.VMEM((1, slots), F32), pltpu.VMEM((lev * TY, TX), F32)],
        2 * TY // 2 * lev * slots * 2 * TX,
        4 << 20,
        got,
    )
    top, bottom = call(
        lon_edge_kernel,
        (shape((lev * HALO, TX), BF),) * 2,
        [],
        2 * lev * 32 * 256 * TX,
        6 << 20,
        own,
        east,
        west,
        band_lon,
    )
    north = [(i, i + 1) for i in range(n_lat - 1)]
    south = [(j, i) for i, j in north]
    above = lax.ppermute(bottom, "lat", north)
    below = lax.ppermute(top, "lat", south)
    middle = call(
        lon_middle_kernel,
        shape((lev * 32, TX), BF),
        [],
        2 * lev * 32 * 256 * TX,
        6 << 20,
        own,
        east,
        west,
        band_lon,
    )
    return call(
        final_kernel,
        shape((levels, TY, TX), BF),
        [pltpu.VMEM((TY * lev, TX), F32), pltpu.VMEM((levels * TY, TX), F32)],
        2 * lev * TY * TX * (TX + levels),
        8 << 20,
        above,
        top,
        middle,
        bottom,
        below,
        band_lat,
        eof_basis,
    )


def solution(mesh):
    in_specs = (P(None, ("lon", "lat")), P(("lon", "lat"), None), P(("lon", "lat")), P(), P())
    out_specs = P(None, "lat", "lon")
    return jax.shard_map(local, mesh=mesh, in_specs=in_specs, out_specs=out_specs, check_vma=False)
```

```python
import jax
import jax.numpy as jnp
from jax import lax
from jax.experimental import pallas as pl
from jax.experimental.pallas import tpu as pltpu
from jax.sharding import PartitionSpec as P

TX = 128
TY = 64
CAP = 128
HALO = 16
SLABS = 8
EDGES = (0, 3)
MIDDLE = (1, 2)
BF = jnp.bfloat16
F32 = jnp.float32
VMEM = pl.BlockSpec(memory_space=pltpu.VMEM)
ANY = pl.BlockSpec(memory_space=pl.ANY)


def tap_table(scale):
    taps = jnp.arange(-15, 16).astype(F32)
    gauss = jnp.exp(-(taps[None, :] * taps[None, :]) / (2.0 * scale[:, None] * scale[:, None]))
    norm = jnp.sqrt(jnp.sum(gauss * gauss, axis=1))
    lane = jnp.arange(TX)
    dist = jnp.minimum(lane, TX - lane).astype(F32)[None, :]
    value = jnp.exp(-(dist * dist) / (2.0 * scale[:, None] * scale[:, None])) / norm[:, None]
    return jnp.where(dist <= 15.0, value, 0.0).astype(BF).astype(F32)


def iota(shape, dim):
    return lax.broadcasted_iota(jnp.int32, shape, dim)


def rows(at, size):
    return pl.ds(pl.multiple_of(at * size, size), size)


def flag(cond):
    return jnp.where(cond, 1.0, 0.0).astype(BF)


def dot_nt(left, right):
    return lax.dot_general(left, right, (((1,), (1,)), ((), ())), preferred_element_type=F32)


def onehot_rows(code, ref):
    spot = iota(ref.shape, 0).astype(F32).astype(BF)
    ref[...] = flag(spot == code.astype(BF))


def bucket_kernel(innov_ref, owner_ref, cell_ref, out_ref, left_ref, right_ref):
    lev, rec = innov_ref.shape
    n_dest = out_ref.shape[0]
    owner = owner_ref[...]
    cell = cell_ref[...]
    padded = (n_dest + 7) // 8 * 8
    hits = jnp.where(iota((padded, rec), 0) == owner, 1.0, 0.0).astype(F32)
    earlier = flag(iota((CAP, CAP), 0) < iota((CAP, CAP), 1))
    carry = jnp.zeros((padded, 1), F32)
    ranks = []
    for block in range(rec // CAP):
        here = hits[:, block * CAP : (block + 1) * CAP]
        before = jnp.dot(here.astype(BF), earlier, preferred_element_type=F32) + carry
        ranks.append(jnp.sum(here * before, axis=0, keepdims=True))
        carry = carry + jnp.sum(here, axis=1, keepdims=True)
    rank = jnp.concatenate(ranks, axis=1)
    onehot_rows(rank + (owner & 1).astype(F32) * float(CAP), right_ref)
    line = iota((16, rec), 0)
    coords = jnp.where(line == 0, cell >> 7, jnp.where(line == 1, cell & 127, 0))
    source = jnp.concatenate([innov_ref[...], coords.astype(F32).astype(BF)], axis=0)
    tall = lev + 16
    pair = (owner >> 1).astype(F32).astype(BF)
    for p in range(n_dest // 2):
        left_ref[p * tall : (p + 1) * tall, :] = source * flag(pair == float(p))
    moved = dot_nt(left_ref[...], right_ref[...]).astype(BF)
    for p in range(n_dest // 2):
        part = moved[p * tall : p * tall + lev + 2]
        out_ref[2 * p] = part[:, :CAP]
        out_ref[2 * p + 1] = part[:, CAP:]


def places(got_ref):
    n_src, lines, _ = got_ref.shape
    row = [got_ref[s, lines - 2 : lines - 1, :].astype(F32) for s in range(n_src)]
    col = [got_ref[s, lines - 1 : lines, :].astype(F32) for s in range(n_src)]
    return (
        jnp.concatenate(row, axis=1).astype(jnp.int32),
        jnp.concatenate(col, axis=1).astype(jnp.int32),
    )


def widen(got_ref, vals_ref):
    n_src, lines, cap = got_ref.shape
    for src in range(n_src):
        vals_ref[:, src * cap : (src + 1) * cap] = got_ref[src, : lines - 2, :].astype(F32)


def edge_kernel(got_ref, first_ref, last_ref, vals_ref, right_ref, left_ref):
    lev, slots = vals_ref.shape
    row, col = places(got_ref)
    widen(got_ref, vals_ref)
    slab = row >> 3
    code = jnp.where(
        col < HALO,
        slab * HALO + col,
        jnp.where(col >= TX - HALO, TX + slab * HALO + col - (TX - HALO), -1),
    )
    onehot_rows(code.astype(F32), right_ref)
    mask = jnp.where(iota((SLABS, slots), 0) == (row & 7), 1.0, 0.0).astype(F32)

    for pair in range(lev // 2):
        both = [
            jnp.broadcast_to(vals_ref[pl.ds(2 * pair + i, 1), :], (SLABS, slots)) * mask
            for i in range(2)
        ]
        left_ref[pair * 16 : (pair + 1) * 16, :] = jnp.concatenate(both, axis=0).astype(BF)

    total = dot_nt(left_ref[...], right_ref[...]).astype(BF)
    first_ref[...] = total[:, :TX]
    last_ref[...] = total[:, TX:]


def spread_kernel(groups, got_ref, out_ref, vals_ref, right_ref, left_ref):
    lev, slots = vals_ref.shape
    row, col = places(got_ref)
    widen(got_ref, vals_ref)
    group = row >> 4
    code = jnp.where(group == groups[0], col, jnp.where(group == groups[1], col + TX, -1))
    onehot_rows(code.astype(F32), right_ref)
    mask = jnp.where(iota((HALO, slots), 0) == (row & 15), 1.0, 0.0).astype(F32)

    for c in range(lev):
        wide = jnp.broadcast_to(vals_ref[pl.ds(c, 1), :], (HALO, slots))
        left_ref[c * HALO : (c + 1) * HALO, :] = (wide * mask).astype(BF)

    total = dot_nt(left_ref[...], right_ref[...]).astype(BF)
    out_ref[0] = total[:, :TX]
    out_ref[1] = total[:, TX:]


def ring_kernel(table_ref, eof_ref, ring_ref, kron_ref):
    lev = table_ref.shape[0]

    @pl.loop(0, lev, unroll=4)
    def _(c):
        base = jnp.broadcast_to(table_ref[pl.ds(c, 1), :], (TX, TX))
        ring_ref[c] = pltpu.roll(base, 0, 1, stride=1, stride_axis=0).astype(BF)

    levels = eof_ref.shape[0]
    wide = lev * 8
    repeat = flag(iota((lev, wide), 0) == iota((lev, wide), 1) >> 3)
    spread_out = jnp.dot(eof_ref[...], repeat, preferred_element_type=F32)
    same = jnp.where(iota((8, wide), 0) == (iota((8, wide), 1) & 7), 1.0, 0.0).astype(F32)
    for level in range(0, levels - 1, 2):
        both = [
            jnp.broadcast_to(spread_out[level + i : level + i + 1], (8, wide)) * same
            for i in range(2)
        ]
        kron_ref[level * 8 : level * 8 + 16, :] = jnp.concatenate(both, axis=0).astype(BF)
    if levels % 2:
        last = jnp.broadcast_to(spread_out[levels - 1 : levels], (8, wide)) * same
        tail = jnp.concatenate([last, jnp.zeros_like(last)], axis=0).astype(BF)
        kron_ref[(levels - 1) * 8 : (levels + 1) * 8, :] = tail


def lon_kernel(groups, own_ref, east_ref, west_ref, ring_ref, out_ref):
    near = flag(jnp.abs(iota((TX, TX), 0) - iota((TX, TX), 1)) < TX // 2)
    far = 1.0 - near
    lane = iota((SLABS, TX), 1)

    def one(c):
        east = east_ref[rows(c, SLABS), :].astype(F32)
        west = west_ref[rows(c, SLABS), :].astype(F32)
        sides = []
        for slab in [2 * g + i for g in groups for i in range(2)]:
            right = pltpu.roll(east, (TX - slab * HALO) % TX, 1)
            left = pltpu.roll(west, (TX - HALO - slab * HALO) % TX, 1)
            sides.append(jnp.where(lane < TX // 2, right, left))
        side = jnp.concatenate(sides, axis=0).astype(BF)
        own = jnp.concatenate([own_ref[i, rows(c, HALO), :] for i in range(2)], axis=0)
        ring = ring_ref[c]
        band = jnp.concatenate([ring * near, ring * far], axis=0)
        return jnp.concatenate([own, side], axis=1), band

    @pl.loop(0, ring_ref.shape[0] // 2, unroll=4)
    def _(pair):
        a, band_a = one(2 * pair)
        b, band_b = one(2 * pair + 1)
        out = jnp.dot(
            jnp.concatenate([a, b], axis=0),
            jnp.concatenate([band_a, band_b], axis=1),
            preferred_element_type=F32,
        ).astype(BF)
        out_ref[0, rows(2 * pair, HALO), :] = out[:HALO, :TX]
        out_ref[1, rows(2 * pair, HALO), :] = out[HALO : 2 * HALO, :TX]
        out_ref[0, rows(2 * pair + 1, HALO), :] = out[2 * HALO : 3 * HALO, TX:]
        out_ref[1, rows(2 * pair + 1, HALO), :] = out[3 * HALO :, TX:]


def mix(kron, lat_ref, out_ref, base):
    levels = kron.shape[0] // 8 - 1
    for i in range(2):
        mixed = jnp.dot(kron, lat_ref[i], preferred_element_type=F32)
        for level in range(levels):
            part = mixed[level * 8 : (level + 1) * 8]
            tile = jnp.concatenate([part[:, :TX], part[:, TX:]], axis=0)
            out_ref[level, base[i] : base[i] + 16, :] = tile.astype(BF)


def store_pair(lat_ref, at, one, two):
    for i in range(2):
        for half in range(2):
            lo = i * 16 + half * 8
            tile = jnp.concatenate([one[lo : lo + 8], two[lo : lo + 8]], axis=0)
            lat_ref[i, rows(at, 16), half * TX : (half + 1) * TX] = tile.astype(BF)


def middle_kernel(edge_ref, middle_ref, ring_ref, kron_ref, out_ref, lat_ref):
    def one(c):
        here = rows(c, HALO)
        field = jnp.concatenate(
            [edge_ref[0, here, :], middle_ref[0, here, :], middle_ref[1, here, :], edge_ref[1, here, :]],
            axis=0,
        )
        return jnp.dot(ring_ref[c, 16:48, :TY], field, preferred_element_type=F32)

    @pl.loop(0, ring_ref.shape[0] // 2, unroll=4)
    def _(pair):
        store_pair(lat_ref, pair, one(2 * pair), one(2 * pair + 1))

    mix(kron_ref[...], lat_ref, out_ref, (0, 16))


def outer_kernel(
    above_ref, edge_ref, middle_ref, below_ref, ring_ref, kron_ref, done_ref, out_ref, lat_ref, mix_ref, sems
):
    copies = [
        pltpu.make_async_copy(done_ref, out_ref.at[:, pl.ds(16, 32), :], sems.at[0]),
        pltpu.make_async_copy(mix_ref.at[0], out_ref.at[:, pl.ds(0, 16), :], sems.at[1]),
        pltpu.make_async_copy(mix_ref.at[1], out_ref.at[:, pl.ds(48, 16), :], sems.at[2]),
    ]
    copies[0].start()

    def one(c):
        here = rows(c, HALO)
        blank = jnp.zeros((TX - TY - 2 * HALO, TX), BF)
        field = jnp.concatenate(
            [
                edge_ref[0, here, :],
                middle_ref[0, here, :],
                middle_ref[1, here, :],
                edge_ref[1, here, :],
                below_ref[here, :],
                blank,
                above_ref[here, :],
            ],
            axis=0,
        )
        taps = jnp.concatenate([ring_ref[c, :16, :], ring_ref[c, 48:64, :]], axis=0)
        return jnp.dot(taps, field, preferred_element_type=F32)

    @pl.loop(0, ring_ref.shape[0] // 2, unroll=4)
    def _(pair):
        store_pair(lat_ref, pair, one(2 * pair), one(2 * pair + 1))

    levels = out_ref.shape[0]
    for i in range(2):
        mixed = jnp.dot(kron_ref[...], lat_ref[i], preferred_element_type=F32)
        for level in range(levels):
            part = mixed[level * 8 : (level + 1) * 8]
            tile = jnp.concatenate([part[:, :TX], part[:, TX:]], axis=0)
            mix_ref[i, level] = tile.astype(BF)
        copies[1 + i].start()
    for copy in copies:
        copy.wait()


def call(kernel, outs, scratch, flops, moved, *args, out_any=False):
    return pl.pallas_call(
        kernel,
        out_shape=outs,
        in_specs=[VMEM] * len(args),
        out_specs=jax.tree.map(lambda _: ANY if out_any else VMEM, outs),
        scratch_shapes=scratch,
        compiler_params=pltpu.CompilerParams(vmem_limit_bytes=32 * 2**20),
        cost_estimate=pl.CostEstimate(flops=flops, bytes_accessed=moved, transcendentals=0),
    )(*args)


def shape(*dims):
    return jax.ShapeDtypeStruct(dims, BF)


def bucket(innovation, owner, cell, n_lon):
    lev, rec = innovation.shape
    tall = n_lon // 2 * (lev + 16)
    scratch = [pltpu.VMEM((tall, rec), BF), pltpu.VMEM((2 * CAP, rec), BF)]
    flops = 2 * tall * rec * 2 * CAP
    return call(
        bucket_kernel, shape(n_lon, lev + 2, CAP), scratch, flops, 1 << 20, innovation, owner, cell
    )


def bound(kernel, groups):
    def inner(*refs):
        kernel(groups, *refs)

    inner.__name__ = kernel.__name__
    return inner


def spread_scratch(lev, slots, part):
    return [
        pltpu.VMEM((lev, slots), F32),
        pltpu.VMEM((2 * TX, slots), BF),
        pltpu.VMEM((part * lev, slots), BF),
    ]


def columns(got):
    n_lon, lines, _ = got.shape
    lev, slots = lines - 2, n_lon * CAP
    flops = 2 * SLABS * lev * slots * 2 * TX
    out = (shape(lev * SLABS, TX),) * 2
    return call(edge_kernel, out, spread_scratch(lev, slots, SLABS), flops, 1 << 20, got)


def spread(got, groups):
    n_lon, lines, _ = got.shape
    lev, slots = lines - 2, n_lon * CAP
    flops = 2 * HALO * lev * slots * 2 * TX
    scratch = spread_scratch(lev, slots, HALO)
    out = shape(2, lev * HALO, TX)
    return call(bound(spread_kernel, groups), out, scratch, flops, 1 << 20, got)


def rings(table, eof):
    lev, levels = table.shape[0], eof.shape[0]
    out = (shape(lev, TX, TX), shape((levels + 1) * 8, lev * 8))
    return call(ring_kernel, out, [], 1 << 26, 4 << 20, table, eof)


def lon_smooth(groups, own, east, west, ring):
    lev = ring.shape[0]
    flops = 2 * lev * 64 * 2 * TX * TX
    out = shape(2, lev * HALO, TX)
    return call(bound(lon_kernel, groups), out, [], flops, 4 << 20, own, east, west, ring)


def finish_middle(edges, middle, ring, kron, levels):
    lev = ring.shape[0]
    scratch = [pltpu.VMEM((2, lev * 8, 2 * TX), BF)]
    flops = 2 * 2 * kron.shape[0] * lev * 8 * 2 * TX
    out = shape(levels, 32, TX)
    return call(middle_kernel, out, scratch, flops, 4 << 20, edges, middle, ring, kron)


def finish(above, edges, middle, below, ring, kron, done):
    lev, levels = ring.shape[0], done.shape[0]
    scratch = [
        pltpu.VMEM((2, lev * 8, 2 * TX), BF),
        pltpu.VMEM((2, levels, HALO, TX), BF),
        pltpu.SemaphoreType.DMA((3,)),
    ]
    flops = 2 * 2 * kron.shape[0] * lev * 8 * 2 * TX
    args = (above, edges, middle, below, ring, kron, done)
    return call(outer_kernel, shape(levels, TY, TX), scratch, flops, 4 << 20, *args, out_any=True)


def local(innovation, owner_tile, cell_index, length_scale, eof_basis):
    n_lon = lax.axis_size("lon")
    n_lat = lax.axis_size("lat")
    levels = eof_basis.shape[0]
    rec = innovation.shape[1]
    sent = bucket(innovation, owner_tile.reshape(1, rec), cell_index.reshape(1, rec), n_lon)
    got = lax.all_to_all(sent, "lon", split_axis=0, concat_axis=0, tiled=True)
    ring, kron = rings(tap_table(length_scale), eof_basis)
    first, last = columns(got)
    up = [(i, (i + 1) % n_lon) for i in range(n_lon)]
    down = [(j, i) for i, j in up]
    west = lax.ppermute(last, "lon", up)
    east = lax.ppermute(first, "lon", down)
    edges = lon_smooth(EDGES, spread(got, EDGES), east, west, ring)
    north = [(i, i + 1) for i in range(n_lat - 1)]
    south = [(j, i) for i, j in north]
    above = lax.ppermute(edges[1], "lat", north)
    below = lax.ppermute(edges[0], "lat", south)
    middle = lon_smooth(MIDDLE, spread(got, MIDDLE), east, west, ring)
    done = finish_middle(edges, middle, ring, kron, levels)
    return finish(above, edges, middle, below, ring, kron, done)


def solution(mesh):
    in_specs = (P(None, ("lon", "lat")), P(("lon", "lat"), None), P(("lon", "lat")), P(), P())
    out_specs = P(None, "lat", "lon")
    return jax.shard_map(local, mesh=mesh, in_specs=in_specs, out_specs=out_specs, check_vma=False)
```

```python
import jax
import jax.numpy as jnp
from jax import lax
from jax.experimental import pallas as pl
from jax.experimental.pallas import tpu as pltpu
from jax.sharding import PartitionSpec as P

TX = 128
TY = 64
CAP = 128
HALO = 16
SLABS = 8
EDGES = (0, 3)
MIDDLE = (1, 2)
BF = jnp.bfloat16
F32 = jnp.float32
VMEM = pl.BlockSpec(memory_space=pltpu.VMEM)
ANY = pl.BlockSpec(memory_space=pl.ANY)
SMEM = pl.BlockSpec(memory_space=pltpu.SMEM)


def tap_table(scale):
    taps = jnp.arange(-15, 16).astype(F32)
    gauss = jnp.exp(-(taps[None, :] * taps[None, :]) / (2.0 * scale[:, None] * scale[:, None]))
    norm = jnp.sqrt(jnp.sum(gauss * gauss, axis=1))
    lane = jnp.arange(TX)
    dist = jnp.minimum(lane, TX - lane).astype(F32)[None, :]
    value = jnp.exp(-(dist * dist) / (2.0 * scale[:, None] * scale[:, None])) / norm[:, None]
    return jnp.where(dist <= 15.0, value, 0.0).astype(BF).astype(F32)


def iota(shape, dim):
    return lax.broadcasted_iota(jnp.int32, shape, dim)


def rows(at, size):
    return pl.ds(pl.multiple_of(at * size, size), size)


def flag(cond):
    return jnp.where(cond, 1.0, 0.0).astype(BF)


def dot_nt(left, right):
    return lax.dot_general(left, right, (((1,), (1,)), ((), ())), preferred_element_type=F32)


def onehot_rows(code, ref):
    spot = iota(ref.shape, 0).astype(F32).astype(BF)
    ref[...] = flag(spot == code.astype(BF))


def bucket_kernel(innov_any, owner_any, cell_any, out_ref, innov_ref, owner_ref, cell_ref, sems, left_ref, right_ref):
    pairs = ((innov_any, innov_ref), (owner_any, owner_ref), (cell_any, cell_ref))
    copies = [pltpu.make_async_copy(*pair, sems.at[i]) for i, pair in enumerate(pairs)]
    for copy in copies:
        copy.start()
    for copy in copies:
        copy.wait()
    lev, rec = innov_ref.shape
    n_dest = out_ref.shape[0]
    owner = owner_ref[...]
    cell = cell_ref[...].reshape(1, rec)
    padded = (n_dest + 7) // 8 * 8
    hits = jnp.where(iota((padded, rec), 0) == owner, 1.0, 0.0).astype(F32)
    earlier = flag(iota((CAP, CAP), 0) < iota((CAP, CAP), 1))
    carry = jnp.zeros((padded, 1), F32)
    ranks = []
    for block in range(rec // CAP):
        here = hits[:, block * CAP : (block + 1) * CAP]
        before = jnp.dot(here.astype(BF), earlier, preferred_element_type=F32) + carry
        ranks.append(jnp.sum(here * before, axis=0, keepdims=True))
        carry = carry + jnp.sum(here, axis=1, keepdims=True)
    rank = jnp.concatenate(ranks, axis=1)
    onehot_rows(rank + (owner & 1).astype(F32) * float(CAP), right_ref)
    line = iota((16, rec), 0)
    coords = jnp.where(line == 0, cell >> 7, jnp.where(line == 1, cell & 127, 0))
    source = jnp.concatenate([innov_ref[...], coords.astype(F32).astype(BF)], axis=0)
    tall = lev + 16
    pair = (owner >> 1).astype(F32).astype(BF)
    for p in range(n_dest // 2):
        left_ref[p * tall : (p + 1) * tall, :] = source * flag(pair == float(p))
    moved = dot_nt(left_ref[...], right_ref[...]).astype(BF)
    for p in range(n_dest // 2):
        part = moved[p * tall : p * tall + lev + 2]
        out_ref[2 * p] = part[:, :CAP]
        out_ref[2 * p + 1] = part[:, CAP:]


def store_swapped(odd_ref, one_ref, two_ref, values):
    @pl.when(odd_ref[0] == 0)
    def _():
        one_ref[...], two_ref[...] = values[0], values[1]

    @pl.when(odd_ref[0] != 0)
    def _():
        one_ref[...], two_ref[...] = values[1], values[0]


def swapped(odd_ref, one, two):
    odd = odd_ref[0] != 0
    return jnp.where(odd, two, one), jnp.where(odd, one, two)


def places(got_ref):
    n_src, lines, _ = got_ref.shape
    row = [got_ref[s, lines - 2 : lines - 1, :].astype(F32) for s in range(n_src)]
    col = [got_ref[s, lines - 1 : lines, :].astype(F32) for s in range(n_src)]
    return (
        jnp.concatenate(row, axis=1).astype(jnp.int32),
        jnp.concatenate(col, axis=1).astype(jnp.int32),
    )


def widen(got_ref, vals_ref):
    n_src, lines, cap = got_ref.shape
    for src in range(n_src):
        vals_ref[:, src * cap : (src + 1) * cap] = got_ref[src, : lines - 2, :].astype(F32)


def edge_kernel(odd_ref, got_ref, one_ref, two_ref, kept_ref, vals_ref, right_ref, left_ref):
    kept_ref[...] = got_ref[...]
    lev, slots = vals_ref.shape
    row, col = places(got_ref)
    widen(got_ref, vals_ref)
    slab = row >> 3
    code = jnp.where(
        col < HALO,
        slab * HALO + col,
        jnp.where(col >= TX - HALO, TX + slab * HALO + col - (TX - HALO), -1),
    )
    onehot_rows(code.astype(F32), right_ref)
    mask = jnp.where(iota((SLABS, slots), 0) == (row & 7), 1.0, 0.0).astype(F32)

    for pair in range(lev // 2):
        both = [
            jnp.broadcast_to(vals_ref[pl.ds(2 * pair + i, 1), :], (SLABS, slots)) * mask
            for i in range(2)
        ]
        left_ref[pair * 16 : (pair + 1) * 16, :] = jnp.concatenate(both, axis=0).astype(BF)

    total = dot_nt(left_ref[...], right_ref[...]).astype(BF)
    store_swapped(odd_ref, one_ref, two_ref, (total[:, TX:], total[:, :TX]))


def spread_kernel(groups, got_ref, out_ref, vals_ref, right_ref, left_ref):
    lev, slots = vals_ref.shape
    row, col = places(got_ref)
    widen(got_ref, vals_ref)
    group = row >> 4
    code = jnp.where(group == groups[0], col, jnp.where(group == groups[1], col + TX, -1))
    onehot_rows(code.astype(F32), right_ref)
    mask = jnp.where(iota((HALO, slots), 0) == (row & 15), 1.0, 0.0).astype(F32)

    for c in range(lev):
        wide = jnp.broadcast_to(vals_ref[pl.ds(c, 1), :], (HALO, slots))
        left_ref[c * HALO : (c + 1) * HALO, :] = (wide * mask).astype(BF)

    total = dot_nt(left_ref[...], right_ref[...]).astype(BF)
    out_ref[0] = total[:, :TX]
    out_ref[1] = total[:, TX:]


def ring_kernel(table_ref, eof_ref, ring_ref, kron_ref):
    lev = table_ref.shape[0]

    @pl.loop(0, lev, unroll=4)
    def _(c):
        base = jnp.broadcast_to(table_ref[pl.ds(c, 1), :], (TX, TX))
        ring_ref[c] = pltpu.roll(base, 0, 1, stride=1, stride_axis=0).astype(BF)

    levels = eof_ref.shape[0]
    wide = lev * 8
    repeat = flag(iota((lev, wide), 0) == iota((lev, wide), 1) >> 3)
    spread_out = jnp.dot(eof_ref[...], repeat, preferred_element_type=F32)
    same = jnp.where(iota((8, wide), 0) == (iota((8, wide), 1) & 7), 1.0, 0.0).astype(F32)
    for level in range(0, levels - 1, 2):
        both = [
            jnp.broadcast_to(spread_out[level + i : level + i + 1], (8, wide)) * same
            for i in range(2)
        ]
        kron_ref[level * 8 : level * 8 + 16, :] = jnp.concatenate(both, axis=0).astype(BF)
    if levels % 2:
        last = jnp.broadcast_to(spread_out[levels - 1 : levels], (8, wide)) * same
        tail = jnp.concatenate([last, jnp.zeros_like(last)], axis=0).astype(BF)
        kron_ref[(levels - 1) * 8 : (levels + 1) * 8, :] = tail


def lon_rows(groups, odd_ref, own_ref, one_ref, two_ref, ring_ref, store):
    near = flag(jnp.abs(iota((TX, TX), 0) - iota((TX, TX), 1)) < TX // 2)
    far = 1.0 - near
    lane = iota((SLABS, TX), 1)

    def one(c):
        east, west = swapped(
            odd_ref,
            one_ref[rows(c, SLABS), :].astype(F32),
            two_ref[rows(c, SLABS), :].astype(F32),
        )
        sides = []
        for slab in [2 * g + i for g in groups for i in range(2)]:
            right = pltpu.roll(east, (TX - slab * HALO) % TX, 1)
            left = pltpu.roll(west, (TX - HALO - slab * HALO) % TX, 1)
            sides.append(jnp.where(lane < TX // 2, right, left))
        side = jnp.concatenate(sides, axis=0).astype(BF)
        own = jnp.concatenate([own_ref[i, rows(c, HALO), :] for i in range(2)], axis=0)
        ring = ring_ref[c]
        band = jnp.concatenate([ring * near, ring * far], axis=0)
        return jnp.concatenate([own, side], axis=1), band

    @pl.loop(0, ring_ref.shape[0] // 2, unroll=4)
    def _(pair):
        a, band_a = one(2 * pair)
        b, band_b = one(2 * pair + 1)
        out = jnp.dot(
            jnp.concatenate([a, b], axis=0),
            jnp.concatenate([band_a, band_b], axis=1),
            preferred_element_type=F32,
        ).astype(BF)
        store(0, rows(2 * pair, HALO), out[:HALO, :TX])
        store(1, rows(2 * pair, HALO), out[HALO : 2 * HALO, :TX])
        store(0, rows(2 * pair + 1, HALO), out[2 * HALO : 3 * HALO, TX:])
        store(1, rows(2 * pair + 1, HALO), out[3 * HALO :, TX:])


def lon_edge_kernel(odd_ref, band_ref, own_ref, one_ref, two_ref, ring_ref, out_ref, far_ref, near_ref):
    def store(group, at, value):
        out_ref[group, at, :] = value

    lon_rows(EDGES, odd_ref, own_ref, one_ref, two_ref, ring_ref, store)
    store_swapped(band_ref, far_ref, near_ref, (out_ref[0], out_ref[1]))


def lon_middle_kernel(odd_ref, own_ref, one_ref, two_ref, ring_ref, out_ref):
    def store(group, at, value):
        out_ref[group, at, :] = value

    lon_rows(MIDDLE, odd_ref, own_ref, one_ref, two_ref, ring_ref, store)


def mix(kron, lat_ref, out_ref, base):
    levels = kron.shape[0] // 8 - 1
    for i in range(2):
        mixed = jnp.dot(kron, lat_ref[i], preferred_element_type=F32)
        for level in range(levels):
            part = mixed[level * 8 : (level + 1) * 8]
            tile = jnp.concatenate([part[:, :TX], part[:, TX:]], axis=0)
            out_ref[level, base[i] : base[i] + 16, :] = tile.astype(BF)


def store_pair(lat_ref, at, one, two):
    for i in range(2):
        for half in range(2):
            lo = i * 16 + half * 8
            tile = jnp.concatenate([one[lo : lo + 8], two[lo : lo + 8]], axis=0)
            lat_ref[i, rows(at, 16), half * TX : (half + 1) * TX] = tile.astype(BF)


def middle_kernel(edge_ref, middle_ref, ring_ref, kron_ref, out_ref, lat_ref):
    def one(c):
        here = rows(c, HALO)
        field = jnp.concatenate(
            [edge_ref[0, here, :], middle_ref[0, here, :], middle_ref[1, here, :], edge_ref[1, here, :]],
            axis=0,
        )
        return jnp.dot(ring_ref[c, 16:48, :TY], field, preferred_element_type=F32)

    @pl.loop(0, ring_ref.shape[0] // 2, unroll=4)
    def _(pair):
        store_pair(lat_ref, pair, one(2 * pair), one(2 * pair + 1))

    mix(kron_ref[...], lat_ref, out_ref, (0, 16))


def outer_kernel(
    band_ref, far_ref, edge_ref, middle_ref, near_ref, ring_ref, kron_ref, done_ref, out_ref, lat_ref, mix_ref, sems
):
    odd = jnp.where(band_ref[0] != 0, 1.0, 0.0).astype(BF)
    even = jnp.where(band_ref[0] != 0, 0.0, 1.0).astype(BF)
    copies = [
        pltpu.make_async_copy(done_ref, out_ref.at[:, pl.ds(16, 32), :], sems.at[0]),
        pltpu.make_async_copy(mix_ref.at[0], out_ref.at[:, pl.ds(0, 16), :], sems.at[1]),
        pltpu.make_async_copy(mix_ref.at[1], out_ref.at[:, pl.ds(48, 16), :], sems.at[2]),
    ]
    copies[0].start()

    def one(c):
        here = rows(c, HALO)
        blank = jnp.zeros((TX - TY - 2 * HALO, TX), BF)
        field = jnp.concatenate(
            [
                edge_ref[0, here, :],
                middle_ref[0, here, :],
                middle_ref[1, here, :],
                edge_ref[1, here, :],
                near_ref[here, :] * even + far_ref[here, :] * odd,
                blank,
                far_ref[here, :] * even + near_ref[here, :] * odd,
            ],
            axis=0,
        )
        taps = jnp.concatenate([ring_ref[c, :16, :], ring_ref[c, 48:64, :]], axis=0)
        return jnp.dot(taps, field, preferred_element_type=F32)

    @pl.loop(0, ring_ref.shape[0] // 2, unroll=4)
    def _(pair):
        store_pair(lat_ref, pair, one(2 * pair), one(2 * pair + 1))

    levels = out_ref.shape[0]
    for i in range(2):
        mixed = jnp.dot(kron_ref[...], lat_ref[i], preferred_element_type=F32)
        for level in range(levels):
            part = mixed[level * 8 : (level + 1) * 8]
            tile = jnp.concatenate([part[:, :TX], part[:, TX:]], axis=0)
            mix_ref[i, level] = tile.astype(BF)
        copies[1 + i].start()
    for copy in copies:
        copy.wait()


def call(kernel, outs, scratch, flops, moved, *args, limit=16, out_any=False, scalars=0):
    return pl.pallas_call(
        kernel,
        out_shape=outs,
        in_specs=[SMEM] * scalars + [VMEM] * (len(args) - scalars),
        out_specs=jax.tree.map(lambda _: ANY if out_any else VMEM, outs),
        scratch_shapes=scratch,
        compiler_params=pltpu.CompilerParams(vmem_limit_bytes=limit * 2**20),
        cost_estimate=pl.CostEstimate(flops=flops, bytes_accessed=moved, transcendentals=0),
    )(*args)


def shape(*dims):
    return jax.ShapeDtypeStruct(dims, BF)


def bucket(innovation, owner, cell, n_lon):
    lev, rec = innovation.shape
    tall = n_lon // 2 * (lev + 16)
    return pl.pallas_call(
        bucket_kernel,
        out_shape=shape(n_lon, lev + 2, CAP),
        in_specs=[pl.BlockSpec(memory_space=pltpu.HBM)] * 3,
        out_specs=VMEM,
        scratch_shapes=[
            pltpu.VMEM((lev, rec), BF),
            pltpu.VMEM((1, rec), jnp.int32),
            pltpu.VMEM((rec,), jnp.int32),
            pltpu.SemaphoreType.DMA((3,)),
            pltpu.VMEM((tall, rec), BF),
            pltpu.VMEM((2 * CAP, rec), BF),
        ],
        compiler_params=pltpu.CompilerParams(vmem_limit_bytes=60 * 2**20),
        cost_estimate=pl.CostEstimate(
            flops=2 * tall * rec * 2 * CAP, bytes_accessed=1 << 20, transcendentals=0
        ),
    )(innovation, owner, cell)


def bound(kernel, groups):
    def inner(*refs):
        kernel(groups, *refs)

    inner.__name__ = kernel.__name__
    return inner


def spread_scratch(lev, slots, part):
    return [
        pltpu.VMEM((lev, slots), F32),
        pltpu.VMEM((2 * TX, slots), BF),
        pltpu.VMEM((part * lev, slots), BF),
    ]


def columns(odd, got):
    n_lon, lines, _ = got.shape
    lev, slots = lines - 2, n_lon * CAP
    flops = 2 * SLABS * lev * slots * 2 * TX
    out = (shape(lev * SLABS, TX), shape(lev * SLABS, TX), shape(*got.shape))
    scratch = spread_scratch(lev, slots, SLABS)
    return call(edge_kernel, out, scratch, flops, 1 << 20, odd, got, scalars=1)


def spread(got, groups):
    n_lon, lines, _ = got.shape
    lev, slots = lines - 2, n_lon * CAP
    flops = 2 * HALO * lev * slots * 2 * TX
    scratch = spread_scratch(lev, slots, HALO)
    out = shape(2, lev * HALO, TX)
    return call(bound(spread_kernel, groups), out, scratch, flops, 1 << 20, got, limit=20)


def rings(table, eof):
    lev, levels = table.shape[0], eof.shape[0]
    out = (shape(lev, TX, TX), shape((levels + 1) * 8, lev * 8))
    return call(ring_kernel, out, [], 1 << 26, 4 << 20, table, eof)


def lon_edges(odd, band, own, one, two, ring):
    lev = ring.shape[0]
    flops = 2 * lev * 64 * 2 * TX * TX
    out = (shape(2, lev * HALO, TX), shape(lev * HALO, TX), shape(lev * HALO, TX))
    args = (odd, band, own, one, two, ring)
    return call(lon_edge_kernel, out, [], flops, 4 << 20, *args, scalars=2)


def lon_middle(odd, own, one, two, ring):
    lev = ring.shape[0]
    flops = 2 * lev * 64 * 2 * TX * TX
    out = shape(2, lev * HALO, TX)
    return call(lon_middle_kernel, out, [], flops, 4 << 20, odd, own, one, two, ring, scalars=1)


def finish_middle(edges, middle, ring, kron, levels):
    lev = ring.shape[0]
    scratch = [pltpu.VMEM((2, lev * 8, 2 * TX), BF)]
    flops = 2 * 2 * kron.shape[0] * lev * 8 * 2 * TX
    out = shape(levels, 32, TX)
    return call(middle_kernel, out, scratch, flops, 4 << 20, edges, middle, ring, kron)


def finish(band, far, edges, middle, near, ring, kron, done):
    lev, levels = ring.shape[0], done.shape[0]
    scratch = [
        pltpu.VMEM((2, lev * 8, 2 * TX), BF),
        pltpu.VMEM((2, levels, HALO, TX), BF),
        pltpu.SemaphoreType.DMA((3,)),
    ]
    flops = 2 * 2 * kron.shape[0] * lev * 8 * 2 * TX
    args = (band, far, edges, middle, near, ring, kron, done)
    return call(outer_kernel, shape(levels, TY, TX), scratch, flops, 4 << 20, *args, out_any=True, scalars=1)


def swaps(axis, ring):
    size = lax.axis_size(axis)
    one = [(i, i + 1) for i in range(0, size - 1, 2)]
    two = [(i, (i + 1) % size) for i in range(1, size if ring else size - 1, 2)]
    return [pairs + [(j, i) for i, j in pairs] for pairs in (one, two)]


def parity(axis):
    return (lax.axis_index(axis) % 2).astype(jnp.int32).reshape(1)


def local(innovation, owner_tile, cell_index, length_scale, eof_basis):
    n_lon = lax.axis_size("lon")
    levels = eof_basis.shape[0]
    rec = innovation.shape[1]
    odd, band = parity("lon"), parity("lat")
    sent = bucket(innovation, owner_tile.reshape(1, rec), cell_index, n_lon)
    got = lax.all_to_all(sent, "lon", split_axis=0, concat_axis=0, tiled=True)
    ring, kron = rings(tap_table(length_scale), eof_basis)
    first, second = swaps("lon", True)
    one, two, got = columns(odd, got)
    one = lax.ppermute(one, "lon", first)
    two = lax.ppermute(two, "lon", second)
    edges, far, near = lon_edges(odd, band, spread(got, EDGES), one, two, ring)
    first, second = swaps("lat", False)
    far = lax.ppermute(far, "lat", second)
    near = lax.ppermute(near, "lat", first)
    middle = lon_middle(odd, spread(got, MIDDLE), one, two, ring)
    done = finish_middle(edges, middle, ring, kron, levels)
    return finish(band, far, edges, middle, near, ring, kron, done)


def solution(mesh):
    in_specs = (P(None, ("lon", "lat")), P(("lon", "lat"), None), P(("lon", "lat")), P(), P())
    out_specs = P(None, "lat", "lon")
    return jax.shard_map(local, mesh=mesh, in_specs=in_specs, out_specs=out_specs, check_vma=False)
```

```python
import jax
import jax.numpy as jnp
from jax import lax
from jax.experimental import pallas as pl
from jax.experimental.pallas import tpu as pltpu
from jax.sharding import PartitionSpec as P

TX = 128
TY = 64
CAP = 128
HALO = 16
EDGES = (0, 3)
MIDDLE = (1, 2)
BF = jnp.bfloat16
F32 = jnp.float32
VMEM = pl.BlockSpec(memory_space=pltpu.VMEM)
ANY = pl.BlockSpec(memory_space=pl.ANY)
SMEM = pl.BlockSpec(memory_space=pltpu.SMEM)


def tap_table(scale):
    taps = jnp.arange(-15, 16).astype(F32)
    gauss = jnp.exp(-(taps[None, :] * taps[None, :]) / (2.0 * scale[:, None] * scale[:, None]))
    norm = jnp.sqrt(jnp.sum(gauss * gauss, axis=1))
    lane = jnp.arange(TX)
    dist = jnp.minimum(lane, TX - lane).astype(F32)[None, :]
    value = jnp.exp(-(dist * dist) / (2.0 * scale[:, None] * scale[:, None])) / norm[:, None]
    return jnp.where(dist <= 15.0, value, 0.0).astype(BF).astype(F32)


def iota(shape, dim):
    return lax.broadcasted_iota(jnp.int32, shape, dim)


def rows(at, size):
    return pl.ds(pl.multiple_of(at * size, size), size)


def flag(cond):
    return jnp.where(cond, 1.0, 0.0).astype(BF)


def dot_nt(left, right):
    return lax.dot_general(left, right, (((1,), (1,)), ((), ())), preferred_element_type=F32)


def onehot_rows(code, ref):
    spot = iota(ref.shape, 0).astype(F32).astype(BF)
    ref[...] = flag(spot == code.astype(BF))


def bucket_kernel(innov_any, owner_any, cell_any, out_ref, innov_ref, owner_ref, cell_ref, sems, left_ref, right_ref):
    pairs = ((innov_any, innov_ref), (owner_any, owner_ref), (cell_any, cell_ref))
    copies = [pltpu.make_async_copy(*pair, sems.at[i]) for i, pair in enumerate(pairs)]
    for copy in copies:
        copy.start()
    copies[1].wait()
    copies[2].wait()
    lev, rec = innov_ref.shape
    n_dest = out_ref.shape[0]
    owner = owner_ref[...]
    cell = cell_ref[...].reshape(1, rec)
    padded = (n_dest + 7) // 8 * 8
    hits = jnp.where(iota((padded, rec), 0) == owner, 1.0, 0.0).astype(F32)
    earlier = flag(iota((CAP, CAP), 0) < iota((CAP, CAP), 1))
    carry = jnp.zeros((padded, 1), F32)
    ranks = []
    for block in range(rec // CAP):
        here = hits[:, block * CAP : (block + 1) * CAP]
        before = jnp.dot(here.astype(BF), earlier, preferred_element_type=F32) + carry
        ranks.append(jnp.sum(here * before, axis=0, keepdims=True))
        carry = carry + jnp.sum(here, axis=1, keepdims=True)
    rank = jnp.concatenate(ranks, axis=1)
    onehot_rows(rank + (owner & 1).astype(F32) * float(CAP), right_ref)
    line = iota((16, rec), 0)
    coords = jnp.where(line == 0, cell >> 7, jnp.where(line == 1, cell & 127, 0))
    copies[0].wait()
    source = jnp.concatenate([innov_ref[...], coords.astype(F32).astype(BF)], axis=0)
    tall = lev + 16
    pair = (owner >> 1).astype(F32).astype(BF)
    for p in range(n_dest // 2):
        left_ref[p * tall : (p + 1) * tall, :] = source * flag(pair == float(p))
    moved = dot_nt(left_ref[...], right_ref[...]).astype(BF)
    for p in range(n_dest // 2):
        part = moved[p * tall : p * tall + lev + 2]
        out_ref[2 * p] = part[:, :CAP]
        out_ref[2 * p + 1] = part[:, CAP:]


def store_swapped(odd_ref, one_ref, two_ref, values):
    @pl.when(odd_ref[0] == 0)
    def _():
        one_ref[...], two_ref[...] = values[0], values[1]

    @pl.when(odd_ref[0] != 0)
    def _():
        one_ref[...], two_ref[...] = values[1], values[0]


def swapped(odd_ref, one, two):
    odd = odd_ref[0] != 0
    return jnp.where(odd, two, one), jnp.where(odd, one, two)


def places(got_ref):
    n_src, lines, _ = got_ref.shape
    row = [got_ref[s, lines - 2 : lines - 1, :].astype(F32) for s in range(n_src)]
    col = [got_ref[s, lines - 1 : lines, :].astype(F32) for s in range(n_src)]
    return (
        jnp.concatenate(row, axis=1).astype(jnp.int32),
        jnp.concatenate(col, axis=1).astype(jnp.int32),
    )


def widen(got_ref, vals_ref):
    n_src, lines, cap = got_ref.shape
    for src in range(n_src):
        vals_ref[:, src * cap : (src + 1) * cap] = got_ref[src, : lines - 2, :].astype(F32)


def spread_rows(groups, got_ref, out_ref, vals_ref, right_ref, left_ref):
    lev, slots = vals_ref.shape
    row, col = places(got_ref)
    widen(got_ref, vals_ref)
    group = row >> 4
    code = jnp.where(group == groups[0], col, jnp.where(group == groups[1], col + TX, -1))
    onehot_rows(code.astype(F32), right_ref)
    mask = jnp.where(iota((HALO, slots), 0) == (row & 15), 1.0, 0.0).astype(F32)

    for c in range(lev):
        wide = jnp.broadcast_to(vals_ref[pl.ds(c, 1), :], (HALO, slots))
        left_ref[c * HALO : (c + 1) * HALO, :] = (wide * mask).astype(BF)

    total = dot_nt(left_ref[...], right_ref[...]).astype(BF)
    out_ref[0] = total[:, :TX]
    out_ref[1] = total[:, TX:]


def edge_kernel(band_ref, got_ref, out_ref, far_ref, near_ref, kept_ref, *scratch):
    kept_ref[...] = got_ref[...]
    spread_rows(EDGES, got_ref, out_ref, *scratch)
    store_swapped(band_ref, far_ref, near_ref, (out_ref[0], out_ref[1]))


def ring_kernel(table_ref, eof_ref, ring_ref, kron_ref):
    lev = table_ref.shape[0]

    @pl.loop(0, lev, unroll=4)
    def _(c):
        base = jnp.broadcast_to(table_ref[pl.ds(c, 1), :], (TX, TX))
        ring_ref[c] = pltpu.roll(base, 0, 1, stride=1, stride_axis=0).astype(BF)

    levels = eof_ref.shape[0]
    wide = lev * 8
    repeat = flag(iota((lev, wide), 0) == iota((lev, wide), 1) >> 3)
    spread_out = jnp.dot(eof_ref[...], repeat, preferred_element_type=F32)
    same = jnp.where(iota((8, wide), 0) == (iota((8, wide), 1) & 7), 1.0, 0.0).astype(F32)
    for level in range(0, levels - 1, 2):
        both = [
            jnp.broadcast_to(spread_out[level + i : level + i + 1], (8, wide)) * same
            for i in range(2)
        ]
        kron_ref[level * 8 : level * 8 + 16, :] = jnp.concatenate(both, axis=0).astype(BF)
    if levels % 2:
        last = jnp.broadcast_to(spread_out[levels - 1 : levels], (8, wide)) * same
        tail = jnp.concatenate([last, jnp.zeros_like(last)], axis=0).astype(BF)
        kron_ref[(levels - 1) * 8 : (levels + 1) * 8, :] = tail


def lat_pass(odd_ref, one, lev, out_ref, one_ref, two_ref):
    lane = iota((8, TX), 1) // HALO

    @pl.loop(0, lev // 4, unroll=2)
    def _(quad):
        firsts, lasts = [], []
        for two in range(2):
            pair = 2 * quad + two
            (taps_a, field_a), (taps_b, field_b) = one(2 * pair), one(2 * pair + 1)
            out = jnp.dot(
                jnp.concatenate([taps_a, taps_b], axis=0),
                jnp.concatenate([field_a, field_b], axis=1),
                preferred_element_type=F32,
            )
            first, last = jnp.zeros((8, TX), F32), jnp.zeros((8, TX), F32)
            for i, part in enumerate((out[:32, :TX], out[32:, TX:])):
                rounded = part.astype(BF)
                out_ref[0, rows(2 * pair + i, HALO), :] = rounded[:HALO]
                out_ref[1, rows(2 * pair + i, HALO), :] = rounded[HALO:]
                for slab in range(4):
                    q = i * 4 + slab
                    turned = part[slab * 8 : slab * 8 + 8]
                    if q:
                        turned = pltpu.roll(turned, q * HALO, 1)
                    first = jnp.where(lane == q, turned, first)
                    last = jnp.where(lane == (q + 7) % 8, turned, last)
            firsts.append(first)
            lasts.append(last)
        one_out, two_out = swapped(
            odd_ref, jnp.concatenate(lasts, axis=0), jnp.concatenate(firsts, axis=0)
        )
        one_ref[rows(quad, 16), :] = one_out.astype(BF)
        two_ref[rows(quad, 16), :] = two_out.astype(BF)


def middle_lat_kernel(odd_ref, got_ref, edge_ref, ring_ref, spread_ref, out_ref, one_ref, two_ref, *scratch):
    spread_rows(MIDDLE, got_ref, spread_ref, *scratch)

    def one(c):
        here = rows(c, HALO)
        parts = [edge_ref[0, here, :], spread_ref[0, here, :], spread_ref[1, here, :], edge_ref[1, here, :]]
        return ring_ref[c, 16:48, :TY], jnp.concatenate(parts, axis=0)

    lat_pass(odd_ref, one, ring_ref.shape[0], out_ref, one_ref, two_ref)


def edge_lat_kernel(
    odd_ref, band_ref, far_ref, edge_ref, spread_ref, near_ref, ring_ref, out_ref, one_ref, two_ref
):
    odd = jnp.where(band_ref[0] != 0, 1.0, 0.0).astype(BF)
    even = jnp.where(band_ref[0] != 0, 0.0, 1.0).astype(BF)
    blank = jnp.zeros((TX - TY - 2 * HALO, TX), BF)

    def one(c):
        here = rows(c, HALO)
        parts = [
            edge_ref[0, here, :],
            spread_ref[0, here, :],
            spread_ref[1, here, :],
            edge_ref[1, here, :],
            near_ref[here, :] * even + far_ref[here, :] * odd,
            blank,
            far_ref[here, :] * even + near_ref[here, :] * odd,
        ]
        taps = jnp.concatenate([ring_ref[c, :16, :], ring_ref[c, 48:64, :]], axis=0)
        return taps, jnp.concatenate(parts, axis=0)

    lat_pass(odd_ref, one, ring_ref.shape[0], out_ref, one_ref, two_ref)


def store_pair(mid_ref, at, one, two):
    for i in range(2):
        for half in range(2):
            lo = i * 16 + half * 8
            tile = jnp.concatenate([one[lo : lo + 8], two[lo : lo + 8]], axis=0)
            mid_ref[i, rows(at, 16), half * TX : (half + 1) * TX] = tile.astype(BF)


def lon_pass(odd_ref, own_ref, one_ref, two_ref, ring_ref, mid_ref):
    near = flag(jnp.abs(iota((TX, TX), 0) - iota((TX, TX), 1)) < TX // 2)
    far = 1.0 - near
    lane = iota((8, TX), 1)

    @pl.loop(0, ring_ref.shape[0] // 4, unroll=2)
    def _(quad):
        easts, wests = swapped(
            odd_ref,
            one_ref[rows(quad, 16), :].astype(F32),
            two_ref[rows(quad, 16), :].astype(F32),
        )
        for two in range(2):
            pair = 2 * quad + two
            east, west = easts[two * 8 : two * 8 + 8], wests[two * 8 : two * 8 + 8]
            fields, bands = [], []
            for i in range(2):
                c = 2 * pair + i
                sides = []
                for slab in range(4):
                    q = i * 4 + slab
                    right = pltpu.roll(east, TX - q * HALO, 1) if q else east
                    left = pltpu.roll(west, TX - q * HALO, 1) if q else west
                    sides.append(jnp.where(lane < TX // 2, right, left))
                side = jnp.concatenate(sides, axis=0).astype(BF)
                own = jnp.concatenate([own_ref[g, rows(c, HALO), :] for g in range(2)], axis=0)
                ring = ring_ref[c]
                fields.append(jnp.concatenate([own, side], axis=1))
                bands.append(jnp.concatenate([ring * near, ring * far], axis=0))
            out = jnp.dot(
                jnp.concatenate(fields, axis=0),
                jnp.concatenate(bands, axis=1),
                preferred_element_type=F32,
            )
            store_pair(mid_ref, pair, out[:32, :TX], out[32:, TX:])


def mix(kron_ref, field, store):
    mixed = jnp.dot(kron_ref[...], field, preferred_element_type=F32)
    for level in range(kron_ref.shape[0] // 8 - 1):
        part = mixed[level * 8 : (level + 1) * 8]
        store(level, jnp.concatenate([part[:, :TX], part[:, TX:]], axis=0).astype(BF))


def middle_lon_kernel(odd_ref, own_ref, one_ref, two_ref, ring_ref, kron_ref, out_ref, mid_ref):
    lon_pass(odd_ref, own_ref, one_ref, two_ref, ring_ref, mid_ref)
    for i in range(2):

        def store(level, tile):
            out_ref[level, i * 16 : i * 16 + 16, :] = tile

        mix(kron_ref, mid_ref[i], store)


def edge_lon_kernel(
    odd_ref, own_ref, one_ref, two_ref, ring_ref, kron_ref, done_ref, out_ref, mid_ref, mix_ref, sems
):
    copies = [
        pltpu.make_async_copy(done_ref, out_ref.at[:, pl.ds(16, 32), :], sems.at[0]),
        pltpu.make_async_copy(mix_ref.at[0], out_ref.at[:, pl.ds(0, 16), :], sems.at[1]),
        pltpu.make_async_copy(mix_ref.at[1], out_ref.at[:, pl.ds(48, 16), :], sems.at[2]),
    ]
    copies[0].start()
    lon_pass(odd_ref, own_ref, one_ref, two_ref, ring_ref, mid_ref)
    for i in range(2):

        def store(level, tile):
            mix_ref[i, level] = tile

        mix(kron_ref, mid_ref[i], store)
        copies[1 + i].start()
    for copy in copies:
        copy.wait()


def call(kernel, outs, scratch, flops, moved, *args, limit=16, out_any=False, scalars=0):
    return pl.pallas_call(
        kernel,
        out_shape=outs,
        in_specs=[SMEM] * scalars + [VMEM] * (len(args) - scalars),
        out_specs=jax.tree.map(lambda _: ANY if out_any else VMEM, outs),
        scratch_shapes=scratch,
        compiler_params=pltpu.CompilerParams(vmem_limit_bytes=limit * 2**20),
        cost_estimate=pl.CostEstimate(flops=flops, bytes_accessed=moved, transcendentals=0),
    )(*args)


def shape(*dims):
    return jax.ShapeDtypeStruct(dims, BF)


def bucket(innovation, owner, cell, n_lon):
    lev, rec = innovation.shape
    tall = n_lon // 2 * (lev + 16)
    return pl.pallas_call(
        bucket_kernel,
        out_shape=shape(n_lon, lev + 2, CAP),
        in_specs=[pl.BlockSpec(memory_space=pltpu.HBM)] * 3,
        out_specs=VMEM,
        scratch_shapes=[
            pltpu.VMEM((lev, rec), BF),
            pltpu.VMEM((1, rec), jnp.int32),
            pltpu.VMEM((rec,), jnp.int32),
            pltpu.SemaphoreType.DMA((3,)),
            pltpu.VMEM((tall, rec), BF),
            pltpu.VMEM((2 * CAP, rec), BF),
        ],
        compiler_params=pltpu.CompilerParams(vmem_limit_bytes=60 * 2**20),
        cost_estimate=pl.CostEstimate(
            flops=2 * tall * rec * 2 * CAP, bytes_accessed=1 << 20, transcendentals=0
        ),
    )(innovation, owner, cell)


def rings(table, eof):
    lev, levels = table.shape[0], eof.shape[0]
    out = (shape(lev, TX, TX), shape((levels + 1) * 8, lev * 8))
    return call(ring_kernel, out, [], 1 << 26, 4 << 20, table, eof)


def spread_scratch(got):
    n_lon, lines, cap = got.shape
    lev, slots = lines - 2, n_lon * cap
    return [
        pltpu.VMEM((lev, slots), F32),
        pltpu.VMEM((2 * TX, slots), BF),
        pltpu.VMEM((HALO * lev, slots), BF),
    ]


def spread_flops(got):
    n_lon, lines, cap = got.shape
    return 2 * HALO * lines * n_lon * cap * 2 * TX


def spread_edges(band, got):
    lev = got.shape[1] - 2
    side = shape(lev * HALO, TX)
    outs = (shape(2, lev * HALO, TX), side, side, shape(*got.shape))
    args = (band, got)
    return call(
        edge_kernel, outs, spread_scratch(got), spread_flops(got), 1 << 20, *args, limit=24, scalars=1
    )


def lat_outs(lev):
    return (shape(2, lev * HALO, TX), shape(lev * 4, TX), shape(lev * 4, TX))


def lat_middle(odd, got, edges, ring):
    lev = ring.shape[0]
    outs = (shape(2, lev * HALO, TX), *lat_outs(lev))
    args = (odd, got, edges, ring)
    return call(
        middle_lat_kernel,
        outs,
        spread_scratch(got),
        spread_flops(got),
        4 << 20,
        *args,
        limit=28,
        scalars=1,
    )


def lat_edges(odd, band, far, edges, middle, near, ring):
    lev = ring.shape[0]
    flops = 4 * lev * 32 * TX * TX
    args = (odd, band, far, edges, middle, near, ring)
    return call(edge_lat_kernel, lat_outs(lev), [], flops, 4 << 20, *args, scalars=2)


def lon_middle(odd, own, one, two, ring, kron, levels):
    lev = ring.shape[0]
    scratch = [pltpu.VMEM((2, lev * 8, 2 * TX), BF)]
    flops = 2 * 2 * kron.shape[0] * lev * 8 * 2 * TX
    out = shape(levels, 32, TX)
    return call(middle_lon_kernel, out, scratch, flops, 4 << 20, odd, own, one, two, ring, kron, scalars=1)


def lon_edges(odd, own, one, two, ring, kron, done):
    lev, levels = ring.shape[0], done.shape[0]
    scratch = [
        pltpu.VMEM((2, lev * 8, 2 * TX), BF),
        pltpu.VMEM((2, levels, HALO, TX), BF),
        pltpu.SemaphoreType.DMA((3,)),
    ]
    flops = 2 * 2 * kron.shape[0] * lev * 8 * 2 * TX
    args = (odd, own, one, two, ring, kron, done)
    return call(edge_lon_kernel, shape(levels, TY, TX), scratch, flops, 4 << 20, *args, out_any=True, scalars=1)


def swaps(axis, ring):
    size = lax.axis_size(axis)
    one = [(i, i + 1) for i in range(0, size - 1, 2)]
    two = [(i, (i + 1) % size) for i in range(1, size if ring else size - 1, 2)]
    return [pairs + [(j, i) for i, j in pairs] for pairs in (one, two)]


def parity(axis):
    return (lax.axis_index(axis) % 2).astype(jnp.int32).reshape(1)


def exchange(axis, ring, one, two):
    first, second = swaps(axis, ring)
    return lax.ppermute(one, axis, first), lax.ppermute(two, axis, second)


def local(innovation, owner_tile, cell_index, length_scale, eof_basis):
    n_lon = lax.axis_size("lon")
    levels = eof_basis.shape[0]
    rec = innovation.shape[1]
    odd, band = parity("lon"), parity("lat")
    sent = bucket(innovation, owner_tile.reshape(1, rec), cell_index, n_lon)
    got = lax.all_to_all(sent, "lon", split_axis=0, concat_axis=0, tiled=True)
    ring, kron = rings(tap_table(length_scale), eof_basis)
    got, ring, kron = lax.optimization_barrier((got, ring, kron))
    edges, far, near, got = spread_edges(band, got)
    near, far = exchange("lat", False, near, far)
    middle, own, one, two = lat_middle(odd, got, edges, ring)
    done = lon_middle(odd, own, *exchange("lon", True, one, two), ring, kron, levels)
    own, one, two = lat_edges(odd, band, far, edges, middle, near, ring)
    return lon_edges(odd, own, *exchange("lon", True, one, two), ring, kron, done)


def solution(mesh):
    in_specs = (P(None, ("lon", "lat")), P(("lon", "lat"), None), P(("lon", "lat")), P(), P())
    out_specs = P(None, "lat", "lon")
    return jax.shard_map(local, mesh=mesh, in_specs=in_specs, out_specs=out_specs, check_vma=False)
```

```python
import jax
import jax.numpy as jnp
from jax import lax
from jax.experimental import pallas as pl
from jax.experimental.pallas import tpu as pltpu
from jax.sharding import PartitionSpec as P

TX = 128
TY = 64
CAP = 128
HALO = 16
SLABS = 8
EDGES = (0, 3)
MIDDLE = (1, 2)
BF = jnp.bfloat16
F32 = jnp.float32
VMEM = pl.BlockSpec(memory_space=pltpu.VMEM)
ANY = pl.BlockSpec(memory_space=pl.ANY)
SMEM = pl.BlockSpec(memory_space=pltpu.SMEM)


def tap_table(scale):
    taps = jnp.arange(-15, 16).astype(F32)
    gauss = jnp.exp(-(taps[None, :] * taps[None, :]) / (2.0 * scale[:, None] * scale[:, None]))
    norm = jnp.sqrt(jnp.sum(gauss * gauss, axis=1))
    lane = jnp.arange(TX)
    dist = jnp.minimum(lane, TX - lane).astype(F32)[None, :]
    value = jnp.exp(-(dist * dist) / (2.0 * scale[:, None] * scale[:, None])) / norm[:, None]
    return jnp.where(dist <= 15.0, value, 0.0).astype(BF).astype(F32)


def iota(shape, dim):
    return lax.broadcasted_iota(jnp.int32, shape, dim)


def rows(at, size):
    return pl.ds(pl.multiple_of(at * size, size), size)


def flag(cond):
    return jnp.where(cond, 1.0, 0.0).astype(BF)


def dot_nt(left, right):
    return lax.dot_general(left, right, (((1,), (1,)), ((), ())), preferred_element_type=F32)


def onehot_rows(code, ref):
    spot = iota(ref.shape, 0).astype(F32).astype(BF)
    ref[...] = flag(spot == code.astype(BF))


def bucket_kernel(innov_any, owner_any, cell_any, out_ref, innov_ref, owner_ref, cell_ref, sems, left_ref, right_ref):
    pairs = ((innov_any, innov_ref), (owner_any, owner_ref), (cell_any, cell_ref))
    copies = [pltpu.make_async_copy(*pair, sems.at[i]) for i, pair in enumerate(pairs)]
    for copy in copies:
        copy.start()
    copies[1].wait()
    copies[2].wait()
    lev, rec = innov_ref.shape
    n_dest = out_ref.shape[0]
    owner = owner_ref[...]
    cell = cell_ref[...].reshape(1, rec)
    padded = (n_dest + 7) // 8 * 8
    hits = jnp.where(iota((padded, rec), 0) == owner, 1.0, 0.0).astype(F32)
    earlier = flag(iota((CAP, CAP), 0) < iota((CAP, CAP), 1))
    carry = jnp.zeros((padded, 1), F32)
    ranks = []
    for block in range(rec // CAP):
        here = hits[:, block * CAP : (block + 1) * CAP]
        before = jnp.dot(here.astype(BF), earlier, preferred_element_type=F32) + carry
        ranks.append(jnp.sum(here * before, axis=0, keepdims=True))
        carry = carry + jnp.sum(here, axis=1, keepdims=True)
    rank = jnp.concatenate(ranks, axis=1)
    onehot_rows(rank + (owner & 1).astype(F32) * float(CAP), right_ref)
    line = iota((16, rec), 0)
    coords = jnp.where(line == 0, cell >> 7, jnp.where(line == 1, cell & 127, 0))
    copies[0].wait()
    source = jnp.concatenate([innov_ref[...], coords.astype(F32).astype(BF)], axis=0)
    tall = lev + 16
    pair = (owner >> 1).astype(F32).astype(BF)
    for p in range(n_dest // 2):
        left_ref[p * tall : (p + 1) * tall, :] = source * flag(pair == float(p))
    moved = dot_nt(left_ref[...], right_ref[...]).astype(BF)
    for p in range(n_dest // 2):
        part = moved[p * tall : p * tall + lev + 2]
        out_ref[2 * p] = part[:, :CAP]
        out_ref[2 * p + 1] = part[:, CAP:]


def store_swapped(odd_ref, one_ref, two_ref, values):
    @pl.when(odd_ref[0] == 0)
    def _():
        one_ref[...], two_ref[...] = values[0], values[1]

    @pl.when(odd_ref[0] != 0)
    def _():
        one_ref[...], two_ref[...] = values[1], values[0]


def swapped(odd_ref, one, two):
    odd = odd_ref[0] != 0
    return jnp.where(odd, two, one), jnp.where(odd, one, two)


def places(got_ref):
    n_src, lines, _ = got_ref.shape
    row = [got_ref[s, lines - 2 : lines - 1, :].astype(F32) for s in range(n_src)]
    col = [got_ref[s, lines - 1 : lines, :].astype(F32) for s in range(n_src)]
    return (
        jnp.concatenate(row, axis=1).astype(jnp.int32),
        jnp.concatenate(col, axis=1).astype(jnp.int32),
    )


def widen(got_ref, vals_ref):
    n_src, lines, cap = got_ref.shape
    for src in range(n_src):
        vals_ref[:, src * cap : (src + 1) * cap] = got_ref[src, : lines - 2, :].astype(F32)


def edge_kernel(odd_ref, got_ref, one_ref, two_ref, kept_ref, vals_ref, right_ref, left_ref):
    kept_ref[...] = got_ref[...]
    lev, slots = vals_ref.shape
    row, col = places(got_ref)
    widen(got_ref, vals_ref)
    slab = row >> 3
    code = jnp.where(
        col < HALO,
        slab * HALO + col,
        jnp.where(col >= TX - HALO, TX + slab * HALO + col - (TX - HALO), -1),
    )
    onehot_rows(code.astype(F32), right_ref)
    mask = jnp.where(iota((SLABS, slots), 0) == (row & 7), 1.0, 0.0).astype(F32)

    for pair in range(lev // 2):
        both = [
            jnp.broadcast_to(vals_ref[pl.ds(2 * pair + i, 1), :], (SLABS, slots)) * mask
            for i in range(2)
        ]
        left_ref[pair * 16 : (pair + 1) * 16, :] = jnp.concatenate(both, axis=0).astype(BF)

    total = dot_nt(left_ref[...], right_ref[...]).astype(BF)
    store_swapped(odd_ref, one_ref, two_ref, (total[:, TX:], total[:, :TX]))


def spread_kernel(groups, got_ref, out_ref, vals_ref, right_ref, left_ref):
    lev, slots = vals_ref.shape
    row, col = places(got_ref)
    widen(got_ref, vals_ref)
    group = row >> 4
    code = jnp.where(group == groups[0], col, jnp.where(group == groups[1], col + TX, -1))
    onehot_rows(code.astype(F32), right_ref)
    mask = jnp.where(iota((HALO, slots), 0) == (row & 15), 1.0, 0.0).astype(F32)

    for c in range(lev):
        wide = jnp.broadcast_to(vals_ref[pl.ds(c, 1), :], (HALO, slots))
        left_ref[c * HALO : (c + 1) * HALO, :] = (wide * mask).astype(BF)

    total = dot_nt(left_ref[...], right_ref[...]).astype(BF)
    out_ref[0] = total[:, :TX]
    out_ref[1] = total[:, TX:]


def spread_edge_kernel(got_ref, ring_ref, own_ref, *scratch):
    *scratch, out_ref = scratch
    spread_kernel(EDGES, got_ref, out_ref, *scratch)
    near = flag(jnp.abs(iota((TX, TX), 0) - iota((TX, TX), 1)) < TX // 2)

    @pl.loop(0, ring_ref.shape[0] // 2, unroll=4)
    def _(pair):
        fields = [out_ref[i, rows(2 * pair + n, HALO), :] for n in range(2) for i in range(2)]
        bands = [ring_ref[2 * pair + n] * near for n in range(2)]
        out = jnp.dot(
            jnp.concatenate(fields, axis=0),
            jnp.concatenate(bands, axis=1),
            preferred_element_type=F32,
        )
        own_ref[rows(2 * pair, 32), :] = out[:32, :TX]
        own_ref[rows(2 * pair + 1, 32), :] = out[32:, TX:]


def ring_kernel(table_ref, eof_ref, ring_ref, kron_ref, tail_ref):
    lev = table_ref.shape[0]
    lane = iota((HALO, TX), 1) // HALO

    @pl.loop(0, lev // 8)
    def _(group):
        for i in range(8):
            base = jnp.broadcast_to(table_ref[pl.ds(group * 8 + i, 1), :], (HALO, TX))
            at = i % 4
            top = pltpu.roll(base, 32 * at + HALO, 1, stride=1, stride_axis=0)
            low = pltpu.roll(base, 32 * at, 1, stride=1, stride_axis=0)
            both = [jnp.where(lane == 2 * at, top, 0.0), jnp.where(lane == 2 * at + 1, low, 0.0)]
            tile = jnp.concatenate(both, axis=0).astype(BF)
            halves = [tile, jnp.zeros_like(tile)]
            here = slice(i * 32, i * 32 + 32)
            tail_ref[group, here, :] = jnp.concatenate(halves if i < 4 else halves[::-1], axis=1)

    @pl.loop(0, lev, unroll=4)
    def _(c):
        base = jnp.broadcast_to(table_ref[pl.ds(c, 1), :], (TX, TX))
        ring_ref[c] = pltpu.roll(base, 0, 1, stride=1, stride_axis=0).astype(BF)

    levels = eof_ref.shape[0]
    wide = lev * 8
    repeat = flag(iota((lev, wide), 0) == iota((lev, wide), 1) >> 3)
    spread_out = jnp.dot(eof_ref[...], repeat, preferred_element_type=F32)
    same = jnp.where(iota((8, wide), 0) == (iota((8, wide), 1) & 7), 1.0, 0.0).astype(F32)
    for level in range(0, levels - 1, 2):
        both = [
            jnp.broadcast_to(spread_out[level + i : level + i + 1], (8, wide)) * same
            for i in range(2)
        ]
        kron_ref[level * 8 : level * 8 + 16, :] = jnp.concatenate(both, axis=0).astype(BF)
    if levels % 2:
        last = jnp.broadcast_to(spread_out[levels - 1 : levels], (8, wide)) * same
        tail = jnp.concatenate([last, jnp.zeros_like(last)], axis=0).astype(BF)
        kron_ref[(levels - 1) * 8 : (levels + 1) * 8, :] = tail


def halo_columns(groups, odd_ref, one_ref, two_ref, c):
    lane = iota((SLABS, TX), 1)
    east, west = swapped(
        odd_ref,
        one_ref[rows(c, SLABS), :].astype(F32),
        two_ref[rows(c, SLABS), :].astype(F32),
    )
    sides = []
    for slab in [2 * g + i for g in groups for i in range(2)]:
        right = pltpu.roll(east, (TX - slab * HALO) % TX, 1)
        left = pltpu.roll(west, (TX - HALO - slab * HALO) % TX, 1)
        sides.append(jnp.where(lane < TX // 2, right, left))
    return jnp.concatenate(sides, axis=0).astype(BF)


def lon_rows(groups, odd_ref, own_ref, one_ref, two_ref, ring_ref, store):
    near = flag(jnp.abs(iota((TX, TX), 0) - iota((TX, TX), 1)) < TX // 2)
    far = 1.0 - near
    lane = iota((SLABS, TX), 1)

    def one(c):
        side = halo_columns(groups, odd_ref, one_ref, two_ref, c)
        own = jnp.concatenate([own_ref[i, rows(c, HALO), :] for i in range(2)], axis=0)
        ring = ring_ref[c]
        band = jnp.concatenate([ring * near, ring * far], axis=0)
        return jnp.concatenate([own, side], axis=1), band

    @pl.loop(0, ring_ref.shape[0] // 2, unroll=4)
    def _(pair):
        a, band_a = one(2 * pair)
        b, band_b = one(2 * pair + 1)
        out = jnp.dot(
            jnp.concatenate([a, b], axis=0),
            jnp.concatenate([band_a, band_b], axis=1),
            preferred_element_type=F32,
        ).astype(BF)
        store(0, rows(2 * pair, HALO), out[:HALO, :TX])
        store(1, rows(2 * pair, HALO), out[HALO : 2 * HALO, :TX])
        store(0, rows(2 * pair + 1, HALO), out[2 * HALO : 3 * HALO, TX:])
        store(1, rows(2 * pair + 1, HALO), out[3 * HALO :, TX:])


def lon_edge_kernel(odd_ref, band_ref, own_ref, one_ref, two_ref, ring_ref, out_ref, far_ref, near_ref):
    far = flag(jnp.abs(iota((TX, TX), 0) - iota((TX, TX), 1)) >= TX // 2)

    @pl.loop(0, ring_ref.shape[0] // 2, unroll=4)
    def _(pair):
        channels = (2 * pair, 2 * pair + 1)
        sides = [halo_columns(EDGES, odd_ref, one_ref, two_ref, c) for c in channels]
        out = jnp.dot(
            jnp.concatenate(sides, axis=0),
            jnp.concatenate([ring_ref[c] * far for c in channels], axis=1),
            preferred_element_type=F32,
        )
        for n, part in enumerate((out[:32, :TX], out[32:, TX:])):
            total = (part + own_ref[rows(channels[n], 32), :]).astype(BF)
            out_ref[0, rows(channels[n], HALO), :] = total[:HALO]
            out_ref[1, rows(channels[n], HALO), :] = total[HALO:]

    store_swapped(band_ref, far_ref, near_ref, (out_ref[0], out_ref[1]))


def lon_middle_kernel(odd_ref, own_ref, one_ref, two_ref, ring_ref, out_ref):
    def store(group, at, value):
        out_ref[group, at, :] = value

    lon_rows(MIDDLE, odd_ref, own_ref, one_ref, two_ref, ring_ref, store)


def mix(kron, lat_ref, out_ref, base):
    levels = kron.shape[0] // 8 - 1
    for i in range(2):
        mixed = jnp.dot(kron, lat_ref[i], preferred_element_type=F32)
        for level in range(levels):
            part = mixed[level * 8 : (level + 1) * 8]
            tile = jnp.concatenate([part[:, :TX], part[:, TX:]], axis=0)
            out_ref[level, base[i] : base[i] + 16, :] = tile.astype(BF)


def store_pair(lat_ref, at, one, two):
    for i in range(2):
        for half in range(2):
            lo = i * 16 + half * 8
            tile = jnp.concatenate([one[lo : lo + 8], two[lo : lo + 8]], axis=0)
            here = slice(at * 16, at * 16 + 16) if isinstance(at, int) else rows(at, 16)
            lat_ref[i, here, half * TX : (half + 1) * TX] = tile.astype(BF)


def middle_kernel(edge_ref, middle_ref, ring_ref, kron_ref, out_ref, part_ref, lat_ref):
    def one(c):
        here = rows(c, HALO)
        field = jnp.concatenate(
            [edge_ref[0, here, :], middle_ref[0, here, :], middle_ref[1, here, :], edge_ref[1, here, :]],
            axis=0,
        )
        out = jnp.dot(ring_ref[c, :TY, :TY], field, preferred_element_type=F32)
        part_ref[rows(c, 32), :] = jnp.concatenate([out[:16], out[48:]], axis=0)
        return out[16:48]

    @pl.loop(0, ring_ref.shape[0] // 2, unroll=4)
    def _(pair):
        store_pair(lat_ref, pair, one(2 * pair), one(2 * pair + 1))

    mix(kron_ref[...], lat_ref, out_ref, (0, 16))


def outer_kernel(
    band_ref, far_ref, near_ref, tail_ref, part_ref, kron_ref, done_ref, out_ref, lat_ref, mix_ref, sems
):
    odd = jnp.where(band_ref[0] != 0, 1.0, 0.0).astype(BF)
    even = jnp.where(band_ref[0] != 0, 0.0, 1.0).astype(BF)
    copies = [
        pltpu.make_async_copy(done_ref, out_ref.at[:, pl.ds(16, 32), :], sems.at[0]),
        pltpu.make_async_copy(mix_ref.at[0], out_ref.at[:, pl.ds(0, 16), :], sems.at[1]),
        pltpu.make_async_copy(mix_ref.at[1], out_ref.at[:, pl.ds(48, 16), :], sems.at[2]),
    ]
    copies[0].start()

    for group in range(tail_ref.shape[0]):
        here = slice(group * 8 * HALO, (group + 1) * 8 * HALO)
        far, near = far_ref[here, :], near_ref[here, :]
        above, below = far * even + near * odd, near * even + far * odd
        halves = [h[i * HALO : (i + 1) * HALO] for i in range(8) for h in (above, below)]
        total = jnp.dot(
            tail_ref[group], jnp.concatenate(halves, axis=0), preferred_element_type=F32
        )
        total = total + part_ref[group * 256 : (group + 1) * 256, :]
        for i in range(4):
            at = i * 64
            store_pair(lat_ref, group * 4 + i, total[at : at + 32], total[at + 32 : at + 64])

    levels = out_ref.shape[0]
    for i in range(2):
        mixed = jnp.dot(kron_ref[...], lat_ref[i], preferred_element_type=F32)
        for level in range(levels):
            part = mixed[level * 8 : (level + 1) * 8]
            tile = jnp.concatenate([part[:, :TX], part[:, TX:]], axis=0)
            mix_ref[i, level] = tile.astype(BF)
        copies[1 + i].start()
    for copy in copies:
        copy.wait()


def call(kernel, outs, scratch, flops, moved, *args, limit=16, out_any=False, scalars=0):
    return pl.pallas_call(
        kernel,
        out_shape=outs,
        in_specs=[SMEM] * scalars + [VMEM] * (len(args) - scalars),
        out_specs=jax.tree.map(lambda _: ANY if out_any else VMEM, outs),
        scratch_shapes=scratch,
        compiler_params=pltpu.CompilerParams(vmem_limit_bytes=limit * 2**20),
        cost_estimate=pl.CostEstimate(flops=flops, bytes_accessed=moved, transcendentals=0),
    )(*args)


def shape(*dims):
    return jax.ShapeDtypeStruct(dims, BF)


def bucket(innovation, owner, cell, n_lon):
    lev, rec = innovation.shape
    tall = n_lon // 2 * (lev + 16)
    return pl.pallas_call(
        bucket_kernel,
        out_shape=shape(n_lon, lev + 2, CAP),
        in_specs=[pl.BlockSpec(memory_space=pltpu.HBM)] * 3,
        out_specs=VMEM,
        scratch_shapes=[
            pltpu.VMEM((lev, rec), BF),
            pltpu.VMEM((1, rec), jnp.int32),
            pltpu.VMEM((rec,), jnp.int32),
            pltpu.SemaphoreType.DMA((3,)),
            pltpu.VMEM((tall, rec), BF),
            pltpu.VMEM((2 * CAP, rec), BF),
        ],
        compiler_params=pltpu.CompilerParams(vmem_limit_bytes=60 * 2**20),
        cost_estimate=pl.CostEstimate(
            flops=2 * tall * rec * 2 * CAP, bytes_accessed=1 << 20, transcendentals=0
        ),
    )(innovation, owner, cell)


def bound(kernel, groups):
    def inner(*refs):
        kernel(groups, *refs)

    inner.__name__ = kernel.__name__
    return inner


def spread_scratch(lev, slots, part):
    return [
        pltpu.VMEM((lev, slots), F32),
        pltpu.VMEM((2 * TX, slots), BF),
        pltpu.VMEM((part * lev, slots), BF),
    ]


def columns(odd, got):
    n_lon, lines, _ = got.shape
    lev, slots = lines - 2, n_lon * CAP
    flops = 2 * SLABS * lev * slots * 2 * TX
    out = (shape(lev * SLABS, TX), shape(lev * SLABS, TX), shape(*got.shape))
    scratch = spread_scratch(lev, slots, SLABS)
    return call(edge_kernel, out, scratch, flops, 1 << 20, odd, got, scalars=1)


def spread(got, groups):
    n_lon, lines, _ = got.shape
    lev, slots = lines - 2, n_lon * CAP
    flops = 2 * HALO * lev * slots * 2 * TX
    scratch = spread_scratch(lev, slots, HALO)
    out = shape(2, lev * HALO, TX)
    return call(bound(spread_kernel, groups), out, scratch, flops, 1 << 20, got, limit=20)


def spread_edges(got, ring):
    n_lon, lines, _ = got.shape
    lev, slots = lines - 2, n_lon * CAP
    flops = 2 * HALO * lev * slots * 2 * TX
    scratch = spread_scratch(lev, slots, HALO) + [pltpu.VMEM((2, lev * HALO, TX), BF)]
    out = jax.ShapeDtypeStruct((lev * 32, TX), F32)
    return call(spread_edge_kernel, out, scratch, flops, 1 << 20, got, ring, limit=24)


def rings(table, eof):
    lev, levels = table.shape[0], eof.shape[0]
    out = (shape(lev, TX, TX), shape((levels + 1) * 8, lev * 8), shape(lev // 8, 256, 256))
    return call(ring_kernel, out, [], 1 << 26, 4 << 20, table, eof)


def lon_edges(odd, band, own, one, two, ring):
    lev = ring.shape[0]
    flops = 2 * lev * 64 * 2 * TX * TX
    out = (shape(2, lev * HALO, TX), shape(lev * HALO, TX), shape(lev * HALO, TX))
    args = (odd, band, own, one, two, ring)
    return call(lon_edge_kernel, out, [], flops, 4 << 20, *args, scalars=2)


def lon_middle(odd, own, one, two, ring):
    lev = ring.shape[0]
    flops = 2 * lev * 64 * 2 * TX * TX
    out = shape(2, lev * HALO, TX)
    return call(lon_middle_kernel, out, [], flops, 4 << 20, odd, own, one, two, ring, scalars=1)


def finish_middle(edges, middle, ring, kron, levels):
    lev = ring.shape[0]
    scratch = [pltpu.VMEM((2, lev * 8, 2 * TX), BF)]
    flops = 2 * 2 * kron.shape[0] * lev * 8 * 2 * TX
    out = (shape(levels, 32, TX), jax.ShapeDtypeStruct((lev * 32, TX), F32))
    return call(middle_kernel, out, scratch, flops, 4 << 20, edges, middle, ring, kron)


def finish(band, far, near, tail, part, kron, done):
    lev, levels = part.shape[0] // 32, done.shape[0]
    scratch = [
        pltpu.VMEM((2, lev * 8, 2 * TX), BF),
        pltpu.VMEM((2, levels, HALO, TX), BF),
        pltpu.SemaphoreType.DMA((3,)),
    ]
    flops = 2 * 2 * kron.shape[0] * lev * 8 * 2 * TX
    args = (band, far, near, tail, part, kron, done)
    return call(outer_kernel, shape(levels, TY, TX), scratch, flops, 4 << 20, *args, out_any=True, scalars=1)


def swaps(axis, ring):
    size = lax.axis_size(axis)
    one = [(i, i + 1) for i in range(0, size - 1, 2)]
    two = [(i, (i + 1) % size) for i in range(1, size if ring else size - 1, 2)]
    return [pairs + [(j, i) for i, j in pairs] for pairs in (one, two)]


def parity(axis):
    return (lax.axis_index(axis) % 2).astype(jnp.int32).reshape(1)


def local(innovation, owner_tile, cell_index, length_scale, eof_basis):
    n_lon = lax.axis_size("lon")
    levels = eof_basis.shape[0]
    rec = innovation.shape[1]
    odd, band = parity("lon"), parity("lat")
    sent = bucket(innovation, owner_tile.reshape(1, rec), cell_index, n_lon)
    got = lax.all_to_all(sent, "lon", split_axis=0, concat_axis=0, tiled=True)
    ring, kron, tail = rings(tap_table(length_scale), eof_basis)
    first, second = swaps("lon", True)
    one, two, got = columns(odd, got)
    one = lax.ppermute(one, "lon", first)
    two = lax.ppermute(two, "lon", second)
    edges, far, near = lon_edges(odd, band, spread_edges(got, ring), one, two, ring)
    first, second = swaps("lat", False)
    far = lax.ppermute(far, "lat", second)
    near = lax.ppermute(near, "lat", first)
    middle = lon_middle(odd, spread(got, MIDDLE), one, two, ring)
    done, part = finish_middle(edges, middle, ring, kron, levels)
    return finish(band, far, near, tail, part, kron, done)


def solution(mesh):
    in_specs = (P(None, ("lon", "lat")), P(("lon", "lat"), None), P(("lon", "lat")), P(), P())
    out_specs = P(None, "lat", "lon")
    return jax.shard_map(local, mesh=mesh, in_specs=in_specs, out_specs=out_specs, check_vma=False)
```

```python
import jax
import jax.numpy as jnp
from jax import lax
from jax.experimental import pallas as pl
from jax.experimental.pallas import tpu as pltpu
from jax.sharding import PartitionSpec as P

TX = 128
TY = 64
CAP = 128
HALO = 16
SLABS = 8
EDGES = (0, 3)
MIDDLE = (1, 2)
BF = jnp.bfloat16
F32 = jnp.float32
VMEM = pl.BlockSpec(memory_space=pltpu.VMEM)
ANY = pl.BlockSpec(memory_space=pl.ANY)
SMEM = pl.BlockSpec(memory_space=pltpu.SMEM)


def tap_table(scale):
    taps = jnp.arange(-15, 16).astype(F32)
    gauss = jnp.exp(-(taps[None, :] * taps[None, :]) / (2.0 * scale[:, None] * scale[:, None]))
    norm = jnp.sqrt(jnp.sum(gauss * gauss, axis=1))
    lane = jnp.arange(TX)
    dist = jnp.minimum(lane, TX - lane).astype(F32)[None, :]
    value = jnp.exp(-(dist * dist) / (2.0 * scale[:, None] * scale[:, None])) / norm[:, None]
    return jnp.where(dist <= 15.0, value, 0.0).astype(BF).astype(F32)


def iota(shape, dim):
    return lax.broadcasted_iota(jnp.int32, shape, dim)


def rows(at, size):
    return pl.ds(pl.multiple_of(at * size, size), size)


def flag(cond):
    return jnp.where(cond, 1.0, 0.0).astype(BF)


def dot_nt(left, right):
    return lax.dot_general(left, right, (((1,), (1,)), ((), ())), preferred_element_type=F32)


def onehot_rows(code, ref):
    spot = iota(ref.shape, 0).astype(F32).astype(BF)
    ref[...] = flag(spot == code.astype(BF))


def bucket_kernel(innov_any, owner_any, cell_any, out_ref, innov_ref, owner_ref, cell_ref, sems, left_ref, right_ref):
    pairs = ((innov_any, innov_ref), (owner_any, owner_ref), (cell_any, cell_ref))
    copies = [pltpu.make_async_copy(*pair, sems.at[i]) for i, pair in enumerate(pairs)]
    for copy in copies:
        copy.start()
    for copy in copies:
        copy.wait()
    lev, rec = innov_ref.shape
    n_dest = out_ref.shape[0]
    owner = owner_ref[...]
    cell = cell_ref[...].reshape(1, rec)
    padded = (n_dest + 7) // 8 * 8
    hits = jnp.where(iota((padded, rec), 0) == owner, 1.0, 0.0).astype(F32)
    earlier = flag(iota((CAP, CAP), 0) < iota((CAP, CAP), 1))
    carry = jnp.zeros((padded, 1), F32)
    ranks = []
    for block in range(rec // CAP):
        here = hits[:, block * CAP : (block + 1) * CAP]
        before = jnp.dot(here.astype(BF), earlier, preferred_element_type=F32) + carry
        ranks.append(jnp.sum(here * before, axis=0, keepdims=True))
        carry = carry + jnp.sum(here, axis=1, keepdims=True)
    rank = jnp.concatenate(ranks, axis=1)
    onehot_rows(rank + (owner & 1).astype(F32) * float(CAP), right_ref)
    line = iota((16, rec), 0)
    coords = jnp.where(line == 0, cell >> 7, jnp.where(line == 1, cell & 127, 0))
    source = jnp.concatenate([innov_ref[...], coords.astype(F32).astype(BF)], axis=0)
    tall = lev + 16
    pair = (owner >> 1).astype(F32).astype(BF)
    for p in range(n_dest // 2):
        left_ref[p * tall : (p + 1) * tall, :] = source * flag(pair == float(p))
    moved = dot_nt(left_ref[...], right_ref[...]).astype(BF)
    for p in range(n_dest // 2):
        part = moved[p * tall : p * tall + lev + 2]
        out_ref[2 * p] = part[:, :CAP]
        out_ref[2 * p + 1] = part[:, CAP:]


def store_swapped(odd_ref, one_ref, two_ref, values):
    @pl.when(odd_ref[0] == 0)
    def _():
        one_ref[...], two_ref[...] = values[0], values[1]

    @pl.when(odd_ref[0] != 0)
    def _():
        one_ref[...], two_ref[...] = values[1], values[0]


def swapped(odd_ref, one, two):
    odd = odd_ref[0] != 0
    return jnp.where(odd, two, one), jnp.where(odd, one, two)


def places(got_ref):
    n_src, lines, _ = got_ref.shape
    row = [got_ref[s, lines - 2 : lines - 1, :].astype(F32) for s in range(n_src)]
    col = [got_ref[s, lines - 1 : lines, :].astype(F32) for s in range(n_src)]
    return (
        jnp.concatenate(row, axis=1).astype(jnp.int32),
        jnp.concatenate(col, axis=1).astype(jnp.int32),
    )


def widen(got_ref, vals_ref):
    n_src, lines, cap = got_ref.shape
    for src in range(n_src):
        vals_ref[:, src * cap : (src + 1) * cap] = got_ref[src, : lines - 2, :].astype(F32)


def edge_kernel(odd_ref, got_ref, one_ref, two_ref, kept_ref, vals_ref, right_ref, left_ref):
    kept_ref[...] = got_ref[...]
    lev, slots = vals_ref.shape
    row, col = places(got_ref)
    widen(got_ref, vals_ref)
    slab = row >> 3
    code = jnp.where(
        col < HALO,
        slab * HALO + col,
        jnp.where(col >= TX - HALO, TX + slab * HALO + col - (TX - HALO), -1),
    )
    onehot_rows(code.astype(F32), right_ref)
    mask = jnp.where(iota((SLABS, slots), 0) == (row & 7), 1.0, 0.0).astype(F32)

    for pair in range(lev // 2):
        both = [
            jnp.broadcast_to(vals_ref[pl.ds(2 * pair + i, 1), :], (SLABS, slots)) * mask
            for i in range(2)
        ]
        left_ref[pair * 16 : (pair + 1) * 16, :] = jnp.concatenate(both, axis=0).astype(BF)

    total = dot_nt(left_ref[...], right_ref[...]).astype(BF)
    store_swapped(odd_ref, one_ref, two_ref, (total[:, TX:], total[:, :TX]))


def spread_kernel(groups, got_ref, out_ref, vals_ref, right_ref, left_ref):
    lev, slots = vals_ref.shape
    row, col = places(got_ref)
    widen(got_ref, vals_ref)
    group = row >> 4
    code = jnp.where(group == groups[0], col, jnp.where(group == groups[1], col + TX, -1))
    onehot_rows(code.astype(F32), right_ref)
    mask = jnp.where(iota((HALO, slots), 0) == (row & 15), 1.0, 0.0).astype(F32)

    for c in range(lev):
        wide = jnp.broadcast_to(vals_ref[pl.ds(c, 1), :], (HALO, slots))
        left_ref[c * HALO : (c + 1) * HALO, :] = (wide * mask).astype(BF)

    total = dot_nt(left_ref[...], right_ref[...]).astype(BF)
    out_ref[0] = total[:, :TX]
    out_ref[1] = total[:, TX:]


def spread_edge_kernel(got_ref, ring_ref, own_ref, *scratch):
    *scratch, out_ref = scratch
    spread_kernel(EDGES, got_ref, out_ref, *scratch)
    near = flag(jnp.abs(iota((TX, TX), 0) - iota((TX, TX), 1)) < TX // 2)

    @pl.loop(0, ring_ref.shape[0] // 2, unroll=4)
    def _(pair):
        fields = [out_ref[i, rows(2 * pair + n, HALO), :] for n in range(2) for i in range(2)]
        bands = [ring_ref[2 * pair + n] * near for n in range(2)]
        out = jnp.dot(
            jnp.concatenate(fields, axis=0),
            jnp.concatenate(bands, axis=1),
            preferred_element_type=F32,
        )
        own_ref[rows(2 * pair, 32), :] = out[:32, :TX]
        own_ref[rows(2 * pair + 1, 32), :] = out[32:, TX:]


def ring_kernel(table_ref, eof_ref, ring_ref, kron_ref, tail_ref):
    lev = table_ref.shape[0]
    lane = iota((HALO, TX), 1) // HALO

    @pl.loop(0, lev // 8)
    def _(group):
        for i in range(8):
            base = jnp.broadcast_to(table_ref[pl.ds(group * 8 + i, 1), :], (HALO, TX))
            at = i % 4
            top = pltpu.roll(base, 32 * at + HALO, 1, stride=1, stride_axis=0)
            low = pltpu.roll(base, 32 * at, 1, stride=1, stride_axis=0)
            both = [jnp.where(lane == 2 * at, top, 0.0), jnp.where(lane == 2 * at + 1, low, 0.0)]
            tile = jnp.concatenate(both, axis=0).astype(BF)
            halves = [tile, jnp.zeros_like(tile)]
            here = slice(i * 32, i * 32 + 32)
            tail_ref[group, here, :] = jnp.concatenate(halves if i < 4 else halves[::-1], axis=1)

    @pl.loop(0, lev, unroll=4)
    def _(c):
        base = jnp.broadcast_to(table_ref[pl.ds(c, 1), :], (TX, TX))
        ring_ref[c] = pltpu.roll(base, 0, 1, stride=1, stride_axis=0).astype(BF)

    levels = eof_ref.shape[0]
    wide = lev * 8
    repeat = flag(iota((lev, wide), 0) == iota((lev, wide), 1) >> 3)
    spread_out = jnp.dot(eof_ref[...], repeat, preferred_element_type=F32)
    same = jnp.where(iota((8, wide), 0) == (iota((8, wide), 1) & 7), 1.0, 0.0).astype(F32)
    for level in range(0, levels - 1, 2):
        both = [
            jnp.broadcast_to(spread_out[level + i : level + i + 1], (8, wide)) * same
            for i in range(2)
        ]
        kron_ref[level * 8 : level * 8 + 16, :] = jnp.concatenate(both, axis=0).astype(BF)
    if levels % 2:
        last = jnp.broadcast_to(spread_out[levels - 1 : levels], (8, wide)) * same
        tail = jnp.concatenate([last, jnp.zeros_like(last)], axis=0).astype(BF)
        kron_ref[(levels - 1) * 8 : (levels + 1) * 8, :] = tail


def halo_columns(groups, odd_ref, one_ref, two_ref, c):
    lane = iota((SLABS, TX), 1)
    east, west = swapped(
        odd_ref,
        one_ref[rows(c, SLABS), :].astype(F32),
        two_ref[rows(c, SLABS), :].astype(F32),
    )
    sides = []
    for slab in [2 * g + i for g in groups for i in range(2)]:
        right = pltpu.roll(east, (TX - slab * HALO) % TX, 1)
        left = pltpu.roll(west, (TX - HALO - slab * HALO) % TX, 1)
        sides.append(jnp.where(lane < TX // 2, right, left))
    return jnp.concatenate(sides, axis=0).astype(BF)


def lon_rows(groups, odd_ref, own_ref, one_ref, two_ref, ring_ref, store):
    near = flag(jnp.abs(iota((TX, TX), 0) - iota((TX, TX), 1)) < TX // 2)
    far = 1.0 - near
    lane = iota((SLABS, TX), 1)

    def one(c):
        side = halo_columns(groups, odd_ref, one_ref, two_ref, c)
        own = jnp.concatenate([own_ref[i, rows(c, HALO), :] for i in range(2)], axis=0)
        ring = ring_ref[c]
        band = jnp.concatenate([ring * near, ring * far], axis=0)
        return jnp.concatenate([own, side], axis=1), band

    @pl.loop(0, ring_ref.shape[0] // 2, unroll=4)
    def _(pair):
        a, band_a = one(2 * pair)
        b, band_b = one(2 * pair + 1)
        out = jnp.dot(
            jnp.concatenate([a, b], axis=0),
            jnp.concatenate([band_a, band_b], axis=1),
            preferred_element_type=F32,
        ).astype(BF)
        store(0, rows(2 * pair, HALO), out[:HALO, :TX])
        store(1, rows(2 * pair, HALO), out[HALO : 2 * HALO, :TX])
        store(0, rows(2 * pair + 1, HALO), out[2 * HALO : 3 * HALO, TX:])
        store(1, rows(2 * pair + 1, HALO), out[3 * HALO :, TX:])


def lon_edge_kernel(odd_ref, band_ref, own_ref, one_ref, two_ref, ring_ref, out_ref, far_ref, near_ref):
    lev = ring_ref.shape[0]
    slab = iota((SLABS, TX), 1) // HALO
    line, lane = iota((HALO, TX), 0), iota((HALO, TX), 1)
    east_far, west_far = flag(lane - line >= TX // 2), flag(line + TX - HALO - lane >= TX // 2)

    def one(c):
        sides = swapped(
            odd_ref,
            one_ref[rows(c, SLABS), :].astype(F32),
            two_ref[rows(c, SLABS), :].astype(F32),
        )
        halves = [
            jnp.concatenate([jnp.where(slab == k, side, 0.0) for k in (0, 1, 6, 7)], axis=0)
            for side in sides
        ]
        east, west = ring_ref[c, :HALO, :] * east_far, ring_ref[c, TX - HALO :, :] * west_far
        taps = jnp.concatenate([east] * SLABS + [west] * SLABS, axis=0)
        return jnp.concatenate(halves, axis=1).astype(BF), taps

    @pl.loop(0, lev // 2, unroll=4)
    def _(pair):
        channels = (2 * pair, 2 * pair + 1)
        (side_a, taps_a), (side_b, taps_b) = one(channels[0]), one(channels[1])
        out = jnp.dot(
            jnp.concatenate([side_a, side_b], axis=0),
            jnp.concatenate([taps_a, taps_b], axis=1),
            preferred_element_type=F32,
        )
        for n, part in enumerate((out[:32, :TX], out[32:, TX:])):
            total = (part + own_ref[rows(channels[n], 32), :]).astype(BF)
            out_ref[0, rows(channels[n], HALO), :] = total[:HALO]
            out_ref[1, rows(channels[n], HALO), :] = total[HALO:]

    def send(group, near_group, unused, first):
        for k in range(lev // HALO):
            at = (lev - lev // HALO + k) * HALO
            rider = out_ref[group, at : at + HALO, :].astype(F32)
            for r in range(HALO - 1):
                here = slice((k * (HALO - 1) + r) * HALO, (k * (HALO - 1) + r + 1) * HALO)
                row = jnp.broadcast_to(rider[first + r : first + r + 1], (HALO, TX))
                block = out_ref[group, here, :].astype(F32)
                far_ref[here, :] = jnp.where(line == unused, row, block).astype(BF)
        near_ref[...] = out_ref[near_group]

    @pl.when(band_ref[0] == 0)
    def _():
        send(0, 1, HALO - 1, 0)

    @pl.when(band_ref[0] != 0)
    def _():
        send(1, 0, 0, 1)


def lon_middle_kernel(odd_ref, own_ref, one_ref, two_ref, ring_ref, out_ref):
    def store(group, at, value):
        out_ref[group, at, :] = value

    lon_rows(MIDDLE, odd_ref, own_ref, one_ref, two_ref, ring_ref, store)


def mix(kron, lat_ref, out_ref, base):
    levels = kron.shape[0] // 8 - 1
    for i in range(2):
        mixed = jnp.dot(kron, lat_ref[i], preferred_element_type=F32)
        for level in range(levels):
            part = mixed[level * 8 : (level + 1) * 8]
            tile = jnp.concatenate([part[:, :TX], part[:, TX:]], axis=0)
            out_ref[level, base[i] : base[i] + 16, :] = tile.astype(BF)


def store_pair(lat_ref, at, one, two):
    for i in range(2):
        for half in range(2):
            lo = i * 16 + half * 8
            tile = jnp.concatenate([one[lo : lo + 8], two[lo : lo + 8]], axis=0)
            here = slice(at * 16, at * 16 + 16) if isinstance(at, int) else rows(at, 16)
            lat_ref[i, here, half * TX : (half + 1) * TX] = tile.astype(BF)


def middle_kernel(edge_ref, middle_ref, ring_ref, kron_ref, out_ref, part_ref, lat_ref):
    def one(c):
        here = rows(c, HALO)
        field = jnp.concatenate(
            [edge_ref[0, here, :], middle_ref[0, here, :], middle_ref[1, here, :], edge_ref[1, here, :]],
            axis=0,
        )
        out = jnp.dot(ring_ref[c, :TY, :TY], field, preferred_element_type=F32)
        part_ref[rows(c, 32), :] = jnp.concatenate([out[:16], out[48:]], axis=0)
        return out[16:48]

    @pl.loop(0, ring_ref.shape[0] // 2, unroll=4)
    def _(pair):
        store_pair(lat_ref, pair, one(2 * pair), one(2 * pair + 1))

    mix(kron_ref[...], lat_ref, out_ref, (0, 16))


def outer_kernel(
    band_ref, far_ref, near_ref, tail_ref, part_ref, kron_ref, done_ref, out_ref, lat_ref, mix_ref, ride_ref, sems
):
    odd = jnp.where(band_ref[0] != 0, 1.0, 0.0).astype(BF)
    even = jnp.where(band_ref[0] != 0, 0.0, 1.0).astype(BF)
    copies = [
        pltpu.make_async_copy(done_ref, out_ref.at[:, pl.ds(16, 32), :], sems.at[0]),
        pltpu.make_async_copy(mix_ref.at[0], out_ref.at[:, pl.ds(0, 16), :], sems.at[1]),
        pltpu.make_async_copy(mix_ref.at[1], out_ref.at[:, pl.ds(48, 16), :], sems.at[2]),
    ]
    copies[0].start()

    lev = part_ref.shape[0] // 32
    kept = lev - lev // HALO
    line = iota((HALO, TX), 0)

    def unload(unused, first):
        for k in range(lev // HALO):
            rider = jnp.zeros((HALO, TX), F32)
            for r in range(HALO - 1):
                at = (k * (HALO - 1) + r) * HALO
                row = far_ref[at : at + HALO, :].astype(F32)[unused : unused + 1]
                rider = jnp.where(line == first + r, jnp.broadcast_to(row, (HALO, TX)), rider)
            ride_ref[k * HALO : (k + 1) * HALO, :] = rider.astype(BF)

    @pl.when(band_ref[0] == 0)
    def _():
        unload(0, 1)

    @pl.when(band_ref[0] != 0)
    def _():
        unload(HALO - 1, 0)

    for group in range(tail_ref.shape[0]):
        halves = []
        for c in range(group * 8, group * 8 + 8):
            ref, at = (far_ref, c * HALO) if c < kept else (ride_ref, (c - kept) * HALO)
            far, near = ref[at : at + HALO, :], near_ref[c * HALO : (c + 1) * HALO, :]
            halves += [far * even + near * odd, near * even + far * odd]
        total = jnp.dot(
            tail_ref[group], jnp.concatenate(halves, axis=0), preferred_element_type=F32
        )
        total = total + part_ref[group * 256 : (group + 1) * 256, :]
        for i in range(4):
            at = i * 64
            store_pair(lat_ref, group * 4 + i, total[at : at + 32], total[at + 32 : at + 64])

    levels = out_ref.shape[0]
    for i in range(2):
        mixed = jnp.dot(kron_ref[...], lat_ref[i], preferred_element_type=F32)
        for level in range(levels):
            part = mixed[level * 8 : (level + 1) * 8]
            tile = jnp.concatenate([part[:, :TX], part[:, TX:]], axis=0)
            mix_ref[i, level] = tile.astype(BF)
        copies[1 + i].start()
    for copy in copies:
        copy.wait()


def call(kernel, outs, scratch, flops, moved, *args, limit=16, out_any=False, scalars=0):
    return pl.pallas_call(
        kernel,
        out_shape=outs,
        in_specs=[SMEM] * scalars + [VMEM] * (len(args) - scalars),
        out_specs=jax.tree.map(lambda _: ANY if out_any else VMEM, outs),
        scratch_shapes=scratch,
        compiler_params=pltpu.CompilerParams(vmem_limit_bytes=limit * 2**20),
        cost_estimate=pl.CostEstimate(flops=flops, bytes_accessed=moved, transcendentals=0),
    )(*args)


def shape(*dims):
    return jax.ShapeDtypeStruct(dims, BF)


def bucket(innovation, owner, cell, n_lon):
    lev, rec = innovation.shape
    tall = n_lon // 2 * (lev + 16)
    return pl.pallas_call(
        bucket_kernel,
        out_shape=shape(n_lon, lev + 2, CAP),
        in_specs=[pl.BlockSpec(memory_space=pltpu.HBM)] * 3,
        out_specs=VMEM,
        scratch_shapes=[
            pltpu.VMEM((lev, rec), BF),
            pltpu.VMEM((1, rec), jnp.int32),
            pltpu.VMEM((rec,), jnp.int32),
            pltpu.SemaphoreType.DMA((3,)),
            pltpu.VMEM((tall, rec), BF),
            pltpu.VMEM((2 * CAP, rec), BF),
        ],
        compiler_params=pltpu.CompilerParams(vmem_limit_bytes=60 * 2**20),
        cost_estimate=pl.CostEstimate(
            flops=2 * tall * rec * 2 * CAP, bytes_accessed=1 << 20, transcendentals=0
        ),
    )(innovation, owner, cell)


def bound(kernel, groups):
    def inner(*refs):
        kernel(groups, *refs)

    inner.__name__ = kernel.__name__
    return inner


def spread_scratch(lev, slots, part):
    return [
        pltpu.VMEM((lev, slots), F32),
        pltpu.VMEM((2 * TX, slots), BF),
        pltpu.VMEM((part * lev, slots), BF),
    ]


def columns(odd, got):
    n_lon, lines, _ = got.shape
    lev, slots = lines - 2, n_lon * CAP
    flops = 2 * SLABS * lev * slots * 2 * TX
    out = (shape(lev * SLABS, TX), shape(lev * SLABS, TX), shape(*got.shape))
    scratch = spread_scratch(lev, slots, SLABS)
    return call(edge_kernel, out, scratch, flops, 1 << 20, odd, got, scalars=1)


def spread(got, groups):
    n_lon, lines, _ = got.shape
    lev, slots = lines - 2, n_lon * CAP
    flops = 2 * HALO * lev * slots * 2 * TX
    scratch = spread_scratch(lev, slots, HALO)
    out = shape(2, lev * HALO, TX)
    return call(bound(spread_kernel, groups), out, scratch, flops, 1 << 20, got, limit=20)


def spread_edges(got, ring):
    n_lon, lines, _ = got.shape
    lev, slots = lines - 2, n_lon * CAP
    flops = 2 * HALO * lev * slots * 2 * TX
    scratch = spread_scratch(lev, slots, HALO) + [pltpu.VMEM((2, lev * HALO, TX), BF)]
    out = jax.ShapeDtypeStruct((lev * 32, TX), F32)
    return call(spread_edge_kernel, out, scratch, flops, 1 << 20, got, ring, limit=24)


def rings(table, eof):
    lev, levels = table.shape[0], eof.shape[0]
    out = (shape(lev, TX, TX), shape((levels + 1) * 8, lev * 8), shape(lev // 8, 256, 256))
    return call(ring_kernel, out, [], 1 << 26, 4 << 20, table, eof)


def lon_edges(odd, band, own, one, two, ring):
    lev = ring.shape[0]
    flops = 2 * lev * 64 * 2 * TX * TX
    sent = (lev - lev // HALO) * HALO
    out = (shape(2, lev * HALO, TX), shape(sent, TX), shape(lev * HALO, TX))
    args = (odd, band, own, one, two, ring)
    return call(lon_edge_kernel, out, [], flops, 4 << 20, *args, scalars=2)


def lon_middle(odd, own, one, two, ring):
    lev = ring.shape[0]
    flops = 2 * lev * 64 * 2 * TX * TX
    out = shape(2, lev * HALO, TX)
    return call(lon_middle_kernel, out, [], flops, 4 << 20, odd, own, one, two, ring, scalars=1)


def finish_middle(edges, middle, ring, kron, levels):
    lev = ring.shape[0]
    scratch = [pltpu.VMEM((2, lev * 8, 2 * TX), BF)]
    flops = 2 * 2 * kron.shape[0] * lev * 8 * 2 * TX
    out = (shape(levels, 32, TX), jax.ShapeDtypeStruct((lev * 32, TX), F32))
    return call(middle_kernel, out, scratch, flops, 4 << 20, edges, middle, ring, kron)


def finish(band, far, near, tail, part, kron, done):
    lev, levels = part.shape[0] // 32, done.shape[0]
    scratch = [
        pltpu.VMEM((2, lev * 8, 2 * TX), BF),
        pltpu.VMEM((2, levels, HALO, TX), BF),
        pltpu.VMEM((lev, TX), BF),
        pltpu.SemaphoreType.DMA((3,)),
    ]
    flops = 2 * 2 * kron.shape[0] * lev * 8 * 2 * TX
    args = (band, far, near, tail, part, kron, done)
    return call(outer_kernel, shape(levels, TY, TX), scratch, flops, 4 << 20, *args, out_any=True, scalars=1)


def swaps(axis, ring):
    size = lax.axis_size(axis)
    one = [(i, i + 1) for i in range(0, size - 1, 2)]
    two = [(i, (i + 1) % size) for i in range(1, size if ring else size - 1, 2)]
    return [pairs + [(j, i) for i, j in pairs] for pairs in (one, two)]


def parity(axis):
    return (lax.axis_index(axis) % 2).astype(jnp.int32).reshape(1)


def local(innovation, owner_tile, cell_index, length_scale, eof_basis):
    n_lon = lax.axis_size("lon")
    levels = eof_basis.shape[0]
    rec = innovation.shape[1]
    odd, band = parity("lon"), parity("lat")
    sent = bucket(innovation, owner_tile.reshape(1, rec), cell_index, n_lon)
    got = lax.all_to_all(sent, "lon", split_axis=0, concat_axis=0, tiled=True)
    ring, kron, tail = rings(tap_table(length_scale), eof_basis)
    first, second = swaps("lon", True)
    one, two, got = columns(odd, got)
    one = lax.ppermute(one, "lon", first)
    two = lax.ppermute(two, "lon", second)
    edges, far, near = lon_edges(odd, band, spread_edges(got, ring), one, two, ring)
    first, second = swaps("lat", False)
    far = lax.ppermute(far, "lat", second)
    near = lax.ppermute(near, "lat", first)
    middle = lon_middle(odd, spread(got, MIDDLE), one, two, ring)
    done, part = finish_middle(edges, middle, ring, kron, levels)
    return finish(band, far, near, tail, part, kron, done)


def solution(mesh):
    in_specs = (P(None, ("lon", "lat")), P(("lon", "lat"), None), P(("lon", "lat")), P(), P())
    out_specs = P(None, "lat", "lon")
    return jax.shard_map(local, mesh=mesh, in_specs=in_specs, out_specs=out_specs, check_vma=False)
```
